32 devices in a mesh: groups: 2 (over y), tile: 4 (over z), mode: 2 (over x), rep: 2 (over core).
Axes of the slice: x: 2, y: 2, z: 4, core: 2. Of those that a mesh axis runs over, the one named last changes fastest.
Arguments:
- object_tiles: bfloat16 [2, 4096, 640], P(None, ('groups', 'tile', 'mode', 'rep')), parts along dimension 1, may hold values from -3 to 3
- probe_modes: bfloat16 [4, 2, 512, 512], P(('groups', 'mode')), parts along dimension 0, may hold values from -3 to 3
- measured: float32 [16, 512, 512], P(('groups', 'tile', 'rep')), parts along dimension 0, may hold values from 0.5 to 3
- row_offset: int32 [16], P(('groups', 'tile', 'rep')), parts along dimension 0, may hold values from 0 to 511
- col_offset: int32 [16], P(('groups', 'tile', 'rep')), parts along dimension 0, may hold values from 0 to 128
Outputs:
- object_grad: float32 [2, 4096, 640], P(None, ('groups', 'tile', 'mode', 'rep')), parts along dimension 1
- probe_grad: float32 [4, 2, 512, 512], P(('groups', 'mode')), parts along dimension 0
The draws below stay inside these ranges and needn't reach their ends.
There are 2 independent parts, one for each index of `groups`. The reference program is written for one: setup_inputs(seed, part) draws one part's arguments, and reference() takes and returns one part's arrays. A program takes and returns all parts, laid end to end along the dimension named above; each array names one. Nothing has to cross between parts.
All inputs are finite; a program needn't handle non-finite values.
Results may differ from the reference program's by a relative error of at most 0.013.
Values may be sent and summed in bfloat16 or wider, within the bound.
A program may use at most 64 MiB of HBM per device.

```python
import math
import jax
import jax.numpy as jnp
from jax import lax

PATCH = 512
COL_EXTRA = 128
TILE_ROWS = 512
OBJ_ROWS = 2048
OBJ_COLS = 640
MODES = 2
POSITIONS = 8
N_REP = 2


def place_ends(entries, key, smallest, high):
    longest = entries.shape.index(max(entries.shape))
    spots = []
    for shift in (0, 1):
        where = [jax.random.randint(jax.random.fold_in(key, axis), (), 0, length) for axis, length in enumerate(entries.shape)]
        where[longest] = (where[longest] + shift) % entries.shape[longest]
        spots.append(tuple(where))
    return entries.at[spots[0]].set(smallest).at[spots[1]].set(high)


def block_scale(key, dims, shards, smallest, high):
    level = 1.0
    for dim, parts in shards:
        draws = jax.random.uniform(jax.random.fold_in(jax.random.fold_in(key, 6), dim), (parts,), jnp.float32, smallest / len(shards), high / len(shards))
        level = level * jnp.repeat(jnp.exp(draws), dims[dim] // parts).reshape((-1,) + (1,) * (len(dims) - 1 - dim))
    return level


def centred(stream_key, extent, deviation, bound, shards=(), kind=jnp.bfloat16):
    level = block_scale(stream_key, extent, shards, -0.22, 0.18) if shards else 1.0
    values = jax.random.normal(stream_key, extent, jnp.float32) * deviation * level
    return jnp.minimum(jnp.maximum(values, -bound), bound).astype(kind)


def setup_inputs(seed: int = 0, part: int = 0) -> dict:
    keys = jax.random.split(jax.random.key(seed), 6)
    part_splits = jax.random.split(jax.random.fold_in(keys[5], part), 6)
    return {
        "object_tiles": centred(part_splits[0], (2, OBJ_ROWS, OBJ_COLS), 0.5, 3.0, ((1, 16),)),
        "probe_modes": centred(part_splits[1], (MODES, 2, PATCH, PATCH), 0.5, 3.0, ((0, 2),)),
        "measured": jnp.clip(jnp.exp(math.log(3.0) - 1.7917595 * jax.random.uniform(part_splits[2], (POSITIONS, PATCH, PATCH), jnp.float32) ** block_scale(part_splits[2], (POSITIONS, PATCH, PATCH), ((0, 8),), -0.2, 0.2)), 0.5, 3.0),
        "row_offset": place_ends(jax.random.randint(part_splits[3], (POSITIONS,), 0, TILE_ROWS), jax.random.fold_in(part_splits[3], 1), 0, TILE_ROWS - 1).astype(jnp.int32),
        "col_offset": place_ends(jax.random.randint(part_splits[4], (POSITIONS,), 0, COL_EXTRA + 1), jax.random.fold_in(part_splits[4], 1), 0, COL_EXTRA).astype(jnp.int32),
    }


def dft_tables(points):
    indices = jnp.arange(points, dtype=jnp.int32)
    products = indices[:, None] * indices[None, :] % points
    angles = products.astype(jnp.float32) * (2.0 * math.pi / points)
    norm_factor = 1.0 / math.sqrt(points)
    cos_table = (jnp.cos(angles) * norm_factor).astype(jnp.bfloat16)
    sin_table = (jnp.sin(angles) * norm_factor).astype(jnp.bfloat16)
    forward_left = jnp.concatenate([jnp.concatenate([cos_table, sin_table], 1), jnp.concatenate([-sin_table, cos_table], 1)], 0)
    inverse_left = jnp.concatenate([jnp.concatenate([cos_table, -sin_table], 1), jnp.concatenate([sin_table, cos_table], 1)], 0)
    return (cos_table, sin_table, forward_left, inverse_left)

def column_pass(left_matrix, stacked):
    points = stacked.shape[-1]
    product = jnp.dot(left_matrix, stacked.reshape(2 * points, points), preferred_element_type=jnp.float32)
    return product.reshape(2, points, points)

def row_pass(stacked, cos_table, sin_table, sign_flip):
    points = stacked.shape[-1]
    flattened = stacked.reshape(2 * points, points)
    with_cos = jnp.dot(flattened, cos_table, preferred_element_type=jnp.float32).reshape(2, points, points)
    with_sin = jnp.dot(flattened, sin_table, preferred_element_type=jnp.float32).reshape(2, points, points)
    real_part = with_cos[0] + sign_flip * with_sin[1]
    imag_part = with_cos[1] - sign_flip * with_sin[0]
    return jnp.stack([real_part, imag_part])

def forward_wave(exit_wave, tables):
    cos_table, sin_table, forward_left, inverse_left = tables
    middle = column_pass(forward_left, exit_wave).astype(jnp.bfloat16)
    return row_pass(middle, cos_table, sin_table, 1.0)

def inverse_wave(corrected, tables):
    cos_table, sin_table, forward_left, inverse_left = tables
    middle = column_pass(inverse_left, corrected).astype(jnp.bfloat16)
    return row_pass(middle, cos_table, sin_table, -1.0)

def complex_times(first, second):
    real_part = first[..., 0, :, :] * second[..., 0, :, :] - first[..., 1, :, :] * second[..., 1, :, :]
    imag_part = first[..., 0, :, :] * second[..., 1, :, :] + first[..., 1, :, :] * second[..., 0, :, :]
    return jnp.stack([real_part, imag_part], axis=-3)

def conj_times(first, second):
    real_part = first[..., 0, :, :] * second[..., 0, :, :] + first[..., 1, :, :] * second[..., 1, :, :]
    imag_part = first[..., 0, :, :] * second[..., 1, :, :] - first[..., 1, :, :] * second[..., 0, :, :]
    return jnp.stack([real_part, imag_part], axis=-3)

def reference(object_tiles, probe_modes, measured, row_offset, col_offset):
    tables = dft_tables(PATCH)
    padding = jnp.zeros((2, TILE_ROWS, OBJ_COLS), object_tiles.dtype)
    extended = jnp.concatenate([object_tiles, padding], axis=1)
    probe_float = probe_modes.astype(jnp.float32)

    def per_position(totals, inputs_now):
        grad_rows, grad_probe = totals
        position, measured_now, row_start, col_start = inputs_now
        zero_index = jnp.zeros((), jnp.int32)
        row_first = (position // N_REP * TILE_ROWS + row_start).astype(jnp.int32)
        col_first = col_start.astype(jnp.int32)
        obj_patch = lax.dynamic_slice(extended, (zero_index, row_first, col_first), (2, PATCH, PATCH)).astype(jnp.float32)
        exit_wave = complex_times(probe_float, obj_patch).astype(jnp.bfloat16)
        spectra = jax.vmap(lambda one_wave: forward_wave(one_wave, tables))(exit_wave)
        intensity = lax.optimization_barrier(jnp.sum(spectra[:, 0] ** 2 + spectra[:, 1] ** 2, axis=0))
        factor = 1.0 - measured_now / jnp.sqrt(jnp.maximum(intensity, 1.0))
        corrected = (spectra * factor).astype(jnp.bfloat16)
        back_wave = jax.vmap(lambda one_wave: inverse_wave(one_wave, tables))(corrected)
        obj_terms = conj_times(probe_float, back_wave)
        obj_terms = lax.optimization_barrier(obj_terms.astype(jnp.bfloat16)).astype(jnp.float32)
        obj_term = lax.optimization_barrier(jnp.sum(obj_terms, axis=0))
        probe_term = conj_times(obj_patch, back_wave)
        index_now = (zero_index, row_first, col_first)
        current = lax.dynamic_slice(grad_rows, index_now, (2, PATCH, PATCH))
        grad_rows = lax.dynamic_update_slice(grad_rows, current + obj_term, index_now)
        return ((grad_rows, grad_probe + probe_term), None)
    start_totals = (jnp.zeros((2, OBJ_ROWS + TILE_ROWS, OBJ_COLS), jnp.float32), jnp.zeros((MODES, 2, PATCH, PATCH), jnp.float32))
    positions = jnp.arange(POSITIONS, dtype=jnp.int32)
    totals, ignored = lax.scan(per_position, start_totals, (positions, measured, row_offset, col_offset))
    grad_rows, grad_probe = totals
    return (grad_rows[:, :OBJ_ROWS], grad_probe)
```

```python
import functools
import math

import jax
import jax.numpy as jnp
import numpy as np
from jax import lax
from jax.experimental import pallas as pl
from jax.experimental.pallas import tpu as pltpu
from jax.sharding import PartitionSpec as P

PATCH = 512
F32, BF16 = jnp.float32, jnp.bfloat16
POWER_ROWS = 128
CHAIN_PARTS = 4

def passed_along(value, axis, steps):
    count = lax.axis_size(axis)
    initial, last = (max(0, -steps), min(count, count - steps))
    return lax.ppermute(value, axis, [(source, source + steps) for source in range(initial, last)])


def dft_tables(points):
    indices = jnp.arange(points, dtype=jnp.int32)
    products = indices[:, None] * indices[None, :] % points
    angles = products.astype(jnp.float32) * (2.0 * math.pi / points)
    norm_factor = 1.0 / math.sqrt(points)
    cos_table = (jnp.cos(angles) * norm_factor).astype(jnp.bfloat16)
    sin_table = (jnp.sin(angles) * norm_factor).astype(jnp.bfloat16)
    forward_left = jnp.concatenate(
        [jnp.concatenate([cos_table, sin_table], 1), jnp.concatenate([-sin_table, cos_table], 1)], 0
    )
    inverse_left = jnp.concatenate(
        [jnp.concatenate([cos_table, -sin_table], 1), jnp.concatenate([sin_table, cos_table], 1)], 0
    )
    return (cos_table, sin_table, forward_left, inverse_left)


def column_pass(left_matrix, stacked):
    points = stacked.shape[-1]
    product = jnp.dot(
        left_matrix, stacked.reshape(2 * points, points), preferred_element_type=jnp.float32
    )
    return product.reshape(2, points, points)


def row_pass(stacked, cos_table, sin_table, sign_flip):
    points = stacked.shape[-1]
    flattened = stacked.reshape(2 * points, points)
    with_cos = jnp.dot(flattened, cos_table, preferred_element_type=jnp.float32).reshape(
        2, points, points
    )
    with_sin = jnp.dot(flattened, sin_table, preferred_element_type=jnp.float32).reshape(
        2, points, points
    )
    real_part = with_cos[0] + sign_flip * with_sin[1]
    imag_part = with_cos[1] - sign_flip * with_sin[0]
    return jnp.stack([real_part, imag_part])


def forward_wave(exit_wave, tables):
    cos_table, sin_table, forward_left, inverse_left = tables
    middle = column_pass(forward_left, exit_wave).astype(jnp.bfloat16)
    return row_pass(middle, cos_table, sin_table, 1.0)


def inverse_wave(corrected, tables):
    cos_table, sin_table, forward_left, inverse_left = tables
    middle = column_pass(inverse_left, corrected).astype(jnp.bfloat16)
    return row_pass(middle, cos_table, sin_table, -1.0)


def complex_times(first, second):
    real_part = first[0] * second[0] - first[1] * second[1]
    imag_part = first[0] * second[1] + first[1] * second[0]
    return jnp.stack([real_part, imag_part])


def conj_times(first, second):
    real_part = first[0] * second[0] + first[1] * second[1]
    imag_part = first[0] * second[1] - first[1] * second[0]
    return jnp.stack([real_part, imag_part])


def local(object_tiles, probe_modes, measured, row_offset, col_offset):
    tables = dft_tables(PATCH)
    own_rows = lax.all_gather(object_tiles, ("mode", "rep"), axis=1, tiled=True)
    next_rows = passed_along(own_rows, "tile", -1)
    extended = jnp.concatenate([own_rows, next_rows], axis=1)
    tile_rows = own_rows.shape[1]
    obj_cols = extended.shape[2]
    zero_index = jnp.zeros((), jnp.int32)
    row_start = row_offset[0]
    col_start = col_offset[0]
    obj_patch = lax.dynamic_slice(
        extended, (zero_index, row_start, col_start), (2, PATCH, PATCH)
    ).astype(jnp.float32)
    probe_float = probe_modes[0].astype(jnp.float32)
    exit_wave = complex_times(probe_float, obj_patch).astype(jnp.bfloat16)
    spectra = forward_wave(exit_wave, tables)
    local_power = spectra[0] ** 2 + spectra[1] ** 2
    intensity = lax.psum(local_power.astype(jnp.bfloat16), "mode").astype(jnp.float32)
    factor = 1.0 - measured[0] / jnp.sqrt(jnp.maximum(intensity, 1.0))
    corrected = (spectra * factor).astype(jnp.bfloat16)
    back_wave = inverse_wave(corrected, tables)
    obj_term = conj_times(probe_float, back_wave).astype(jnp.bfloat16).astype(jnp.float32)
    extended_term = jnp.zeros((2, 2 * tile_rows, obj_cols), jnp.float32)
    extended_term = lax.dynamic_update_slice(
        extended_term, obj_term, (zero_index, row_start, col_start)
    )
    own_sum, next_sum = (
        lax.psum_scatter(
            extended_term[:, :tile_rows].astype(jnp.bfloat16),
            ("mode", "rep"),
            scatter_dimension=1,
            tiled=True,
        ).astype(jnp.float32),
        lax.psum_scatter(
            extended_term[:, tile_rows:].astype(jnp.bfloat16),
            ("mode", "rep"),
            scatter_dimension=1,
            tiled=True,
        ).astype(jnp.float32),
    )
    carried = passed_along(next_sum.astype(jnp.bfloat16), "tile", 1).astype(next_sum.dtype)
    object_grad = own_sum + carried
    probe_term = conj_times(obj_patch, back_wave)
    probe_grad = lax.psum(probe_term.astype(jnp.bfloat16), ("tile", "rep")).astype(jnp.float32)
    return (object_grad, probe_grad[None])


def cos_sin_tables(points):
    products = np.outer(np.arange(points), np.arange(points)) % points
    angles = products * (2.0 * math.pi / points)
    norm_factor = 1.0 / math.sqrt(points)
    return (
        (np.cos(angles) * norm_factor).astype(jnp.bfloat16),
        (np.sin(angles) * norm_factor).astype(jnp.bfloat16),
    )


def matmul(left, right):
    return jnp.dot(left, right, preferred_element_type=F32)


def rows_at(start, size):
    return pl.ds(pl.multiple_of(start, size), size)


def fused_kernel(
    tiles, row_ref, col_ref, obj, probe, cos_ref, sin_ref, measured, object_out, probe_out,
    ext, shift_out, shift_in, rotate, rotate_back, left_fwd, right_fwd, right_inv, left_inv,
    probe_rot, patch, wave, middle, spec, power, power_in, back_stack, term, term_in,
    probe_term, half_out, half_in, half_sum, up_left, up_right, up_out, down, down_in,
    placed_out, placed_mine, placed_in, carry_out, carry_in,
    g_send, g_recv, s_send, s_recv, pw_send, pw_recv, t_send, t_recv, h_send, h_recv,
    up_send, up_recv, dn_send, dn_recv, sib_send, sib_recv, pl_send, pl_recv, c_send, c_recv,
):
    t, m, r = lax.axis_index("tile"), lax.axis_index("mode"), lax.axis_index("rep")
    sibling, partner = {"rep": 1 - r}, {"mode": 1 - m}
    lower, upper = {"tile": t - 1}, {"tile": t + 1}
    has_lower, has_upper = t > 0, t < tiles - 1
    height, width = obj.shape[1], obj.shape[2]
    points = probe.shape[-1]
    row_start, col_start = row_ref[0], col_ref[0]

    def copy(src, dst, send, recv, device):
        return pltpu.make_async_remote_copy(
            src_ref=src, dst_ref=dst, send_sem=send, recv_sem=recv,
            device_id=device, device_id_type=pl.DeviceIdType.MESH,
        )

    barrier = pltpu.get_barrier_semaphore()
    for device in (sibling, partner):
        pl.semaphore_signal(barrier, inc=1, device_id=device, device_id_type=pl.DeviceIdType.MESH)

    @pl.when(has_lower)
    def _():
        pl.semaphore_signal(barrier, inc=1, device_id=lower, device_id_type=pl.DeviceIdType.MESH)

    @pl.when(has_upper)
    def _():
        pl.semaphore_signal(barrier, inc=1, device_id=upper, device_id_type=pl.DeviceIdType.MESH)

    peers = 2 + has_lower.astype(jnp.int32) + has_upper.astype(jnp.int32)
    pl.semaphore_wait(barrier, peers)

    own_slot, other_slot = 2 * m + r, 2 * (1 - m) + r

    def gather(kind, part, src, slot, device):
        return copy(src, ext.at[slot, part], g_send.at[kind, part], g_recv.at[kind, part], device)

    def block(slot, part):
        return ext.at[slot, part]

    def to_sibling(part):
        return gather(0, part, obj.at[part], own_slot, sibling)

    def to_partner(part):
        return gather(1, part, obj.at[part], own_slot, partner)

    def to_lower(part):
        return gather(2, part, obj.at[part], 4 + own_slot, lower)

    def relay_partner(part):
        return gather(3, part, block(other_slot, part), other_slot, sibling)

    def relay_upper(part):
        return gather(4, part, block(4 + own_slot, part), 4 + own_slot, sibling)

    def cross_partner(part):
        return gather(5, part, block(4 + own_slot, part), 4 + own_slot, partner)

    def cross_lower(part):
        return gather(5, part, block(other_slot, part), 4 + other_slot, lower)

    def relay_cross(part):
        return gather(6, part, block(4 + other_slot, part), 4 + other_slot, sibling)

    for part in range(2):
        to_partner(part).start()

        @pl.when(has_lower)
        def _():
            to_lower(part).start()

        to_sibling(part).start()
    shift_out[...] = jnp.full(shift_out.shape, row_start, jnp.int32)
    send_shift = copy(shift_out, shift_in, s_send, s_recv, sibling)
    send_shift.start()

    first = lax.broadcasted_iota(jnp.int32, (points, points), 0)
    second = lax.broadcasted_iota(jnp.int32, (points, points), 1)
    apart = first - second - row_start
    rotate[...] = jnp.where((apart == 0) | (apart == -points), 1.0, 0.0).astype(BF16)
    apart = second - first - row_start
    rotate_back[...] = jnp.where((apart == 0) | (apart == -points), 1.0, 0.0).astype(BF16)
    cosine, sine = cos_ref[...], sin_ref[...]
    minus = -sine
    right_fwd[:points, :points] = cosine
    right_fwd[:points, points:] = minus
    right_fwd[points:, :points] = sine
    right_fwd[points:, points:] = cosine
    right_inv[:points, :points] = cosine
    right_inv[:points, points:] = sine
    right_inv[points:, :points] = minus
    right_inv[points:, points:] = cosine

    @pl.loop(0, 4)
    def _(step):
        rows = rows_at(step * 128, 128)
        low = rows_at(points + step * 128, 128)
        turn = rotate[rows, :]
        cos_rot = matmul(turn, cos_ref[...]).astype(BF16)
        sin_rot = matmul(turn, sin_ref[...]).astype(BF16)
        left_inv[rows, :points] = cos_rot
        left_inv[rows, points:] = -sin_rot
        left_inv[low, :points] = sin_rot
        left_inv[low, points:] = cos_rot
        cos_turn = matmul(cos_ref[rows, :], rotate_back[...]).astype(BF16)
        sin_turn = matmul(sin_ref[rows, :], rotate_back[...]).astype(BF16)
        left_fwd[rows, :points] = cos_turn
        left_fwd[rows, points:] = sin_turn
        left_fwd[low, :points] = -sin_turn
        left_fwd[low, points:] = cos_turn
        for part in range(2):
            probe_rot[part, rows, :] = matmul(turn, probe[0, part]).astype(BF16)

    ext[own_slot] = obj[...]

    @pl.when(jnp.logical_not(has_upper))
    def _():
        ext[4:8] = jnp.zeros((4, 2, height, width), BF16)

    @pl.when(t == 0)
    def _():
        up_left[...] = jnp.zeros_like(up_left)

    @pl.when(t == tiles - 1)
    def _():
        up_right[...] = jnp.zeros_like(up_right)

    for part in range(2):
        gather(1, part, obj.at[part], other_slot, partner).wait_recv()
        relay_partner(part).start()

        @pl.when((r == 1) & has_lower)
        def _():
            cross_lower(part).start()

        @pl.when(has_upper)
        def _():
            gather(2, part, obj.at[part], 4 + own_slot, lower).wait_recv()
            relay_upper(part).start()

            @pl.when(r == 0)
            def _():
                cross_partner(part).start()

    for part in range(2):
        @pl.when(has_upper)
        def _():
            gather(5, part, obj.at[part], 4 + other_slot, partner).wait_recv()
            relay_cross(part).start()

    for part in range(2):
        to_sibling(part).wait()
        to_partner(part).wait_send()
        relay_partner(part).wait()

        @pl.when(has_lower)
        def _():
            to_lower(part).wait_send()

        @pl.when((r == 1) & has_lower)
        def _():
            cross_lower(part).wait_send()

        @pl.when(has_upper)
        def _():
            relay_upper(part).wait()
            relay_cross(part).wait()

        @pl.when((r == 0) & has_upper)
        def _():
            cross_partner(part).wait_send()

    pick = lax.broadcasted_iota(jnp.int32, (width, points), 0) - lax.broadcasted_iota(
        jnp.int32, (width, points), 1
    )
    pick = jnp.where(pick == col_start, 1.0, 0.0).astype(BF16)

    @pl.loop(0, 4)
    def _(step):
        rows = rows_at(step * height, height)
        low = rows_at(points + step * height, height)
        line = lax.broadcasted_iota(jnp.int32, (height, width), 0) + step * height
        parts = []
        for part in range(2):
            chosen = jnp.where(
                line >= row_start, ext[step, part].astype(F32), ext[4 + step, part].astype(F32)
            )
            parts.append(matmul(chosen.astype(BF16), pick))
            patch[part, rows, :] = parts[part].astype(BF16)
        obj_re, obj_im = parts
        prb_re, prb_im = (probe_rot[part, rows, :].astype(F32) for part in range(2))
        wave[rows, :] = (prb_re * obj_re - prb_im * obj_im).astype(BF16)
        wave[low, :] = (prb_re * obj_im + prb_im * obj_re).astype(BF16)

    @pl.loop(0, 2)
    def _(step):
        rows = rows_at(step * 256, 256)
        low = rows_at(points + step * 256, 256)
        middle[rows, :points] = matmul(left_fwd[rows, :], wave[...]).astype(BF16)
        middle[rows, points:] = matmul(left_fwd[low, :], wave[...]).astype(BF16)

    def send_power(step):
        return copy(
            power.at[step], power_in.at[step], pw_send.at[step], pw_recv.at[step], partner
        )

    steps = points // POWER_ROWS

    @pl.loop(0, steps)
    def _(step):
        rows = rows_at(step * POWER_ROWS, POWER_ROWS)
        wide = matmul(middle[rows, :], right_fwd[...])
        spec[rows, :] = wide
        power[step] = (wide[:, :points] ** 2 + wide[:, points:] ** 2).astype(BF16)
        send_power(step).start()

    @pl.loop(0, steps)
    def _(step):
        rows = rows_at(step * POWER_ROWS, POWER_ROWS)
        low = rows_at(points + step * POWER_ROWS, POWER_ROWS)
        send_power(step).wait()
        spec_re, spec_im = spec[rows, :points], spec[rows, points:]
        intensity = spec_re**2 + spec_im**2 + power_in[step].astype(F32)
        factor = 1.0 - measured[0, rows, :] / jnp.sqrt(jnp.maximum(intensity, 1.0))
        corrected = jnp.concatenate(
            [(spec_re * factor).astype(BF16), (spec_im * factor).astype(BF16)], 1
        )
        turned = matmul(corrected, right_inv[...]).astype(BF16)
        back_stack[rows, :] = turned[:, :points]
        back_stack[low, :] = turned[:, points:]

    def send_term(step):
        return copy(
            term.at[2 * (1 - m) + step], term_in.at[step], t_send.at[step], t_recv.at[step], partner
        )

    @pl.loop(0, 4)
    def _(step):
        slot = (step + 2 * (1 - m)) % 4
        rows = rows_at(slot * height, height)
        low = rows_at(points + slot * height, height)
        back_re = matmul(left_inv[rows, :], back_stack[...])
        back_im = matmul(left_inv[low, :], back_stack[...])
        prb_re, prb_im = (probe_rot[part, rows, :].astype(F32) for part in range(2))
        term[slot, 0] = (prb_re * back_re + prb_im * back_im).astype(BF16)
        term[slot, 1] = (prb_re * back_im - prb_im * back_re).astype(BF16)

        @pl.when(step < 2)
        def _():
            send_term(step).start()

        obj_re, obj_im = (patch[part, rows, :].astype(F32) for part in range(2))
        probe_term[rows, :points] = (obj_re * back_re + obj_im * back_im).astype(BF16)
        probe_term[rows, points:] = (obj_re * back_im - obj_im * back_re).astype(BF16)

    half = points // 2
    chunk = half // CHAIN_PARTS
    half_out[...] = matmul(rotate_back[rows_at((1 - r) * half, half), :], probe_term[...]).astype(BF16)
    send_half = copy(half_out, half_in, h_send, h_recv, sibling)
    send_half.start()
    half_sum[...] = matmul(rotate_back[rows_at(r * half, half), :], probe_term[...])
    send_half.wait()
    half_sum[...] += half_in[...].astype(F32)
    root = tiles // 2

    def part_rows(index):
        return pl.ds(index * chunk, chunk)

    def up_to_upper(index):
        rows = part_rows(index)
        return copy(up_out.at[rows], up_left.at[rows], up_send.at[index], up_recv.at[0, index], upper)

    def up_to_lower(index):
        rows = part_rows(index)
        return copy(up_out.at[rows], up_right.at[rows], up_send.at[index], up_recv.at[1, index], lower)

    def down_to_upper(index):
        rows = part_rows(index)
        return copy(down.at[rows], down.at[rows], dn_send.at[0, index], dn_recv.at[index], upper)

    def down_to_lower(index):
        rows = part_rows(index)
        return copy(down.at[rows], down.at[rows], dn_send.at[1, index], dn_recv.at[index], lower)

    def down_to_sibling(index):
        rows = part_rows(index)
        return copy(down.at[rows], down_in.at[rows], sib_send.at[index], sib_recv.at[index], sibling)

    for index in range(CHAIN_PARTS):
        rows = part_rows(index)

        @pl.when((t <= root) & has_lower)
        def _():
            up_to_upper(index).wait_recv()

        @pl.when((t >= root) & has_upper)
        def _():
            up_to_lower(index).wait_recv()

        @pl.when(t < root)
        def _():
            up_out[rows] = (half_sum[rows] + up_left[rows].astype(F32)).astype(BF16)
            up_to_upper(index).start()

        @pl.when(t > root)
        def _():
            up_out[rows] = (half_sum[rows] + up_right[rows].astype(F32)).astype(BF16)
            up_to_lower(index).start()

        @pl.when(t == root)
        def _():
            down[rows] = (
                half_sum[rows] + up_left[rows].astype(F32) + up_right[rows].astype(F32)
            ).astype(BF16)

            @pl.when(has_lower)
            def _():
                down_to_lower(index).start()

            @pl.when(has_upper)
            def _():
                down_to_upper(index).start()

            down_to_sibling(index).start()

    place = lax.broadcasted_iota(jnp.int32, (points, width), 1) - lax.broadcasted_iota(
        jnp.int32, (points, width), 0
    )
    place = jnp.where(place == col_start, 1.0, 0.0).astype(BF16)
    send_placed = copy(placed_out, placed_in, pl_send, pl_recv, sibling)
    for step in range(2):
        send_term(step).wait()
    for step in range(2):
        which = 1 - r if step == 0 else r
        for part in range(2):
            total = term[2 * m + which, part].astype(F32) + term_in[which, part].astype(F32)
            spread = matmul(total.astype(BF16), place).astype(BF16)
            if step == 0:
                placed_out[part] = spread
            else:
                placed_mine[part] = spread
        if step == 0:
            send_placed.start()
    send_shift.wait()
    send_placed.wait()
    shift = shift_in[0:1, :]
    shift = jnp.broadcast_to(jnp.concatenate([shift] * (width // 128), 1), (height, width))
    line = lax.broadcasted_iota(jnp.int32, (height, width), 0) + own_slot * height
    zero = jnp.zeros((height, width), F32)
    send_carry = copy(carry_out, carry_in, c_send, c_recv, upper)
    for part in range(2):
        mine, theirs = placed_mine[part].astype(F32), placed_in[part].astype(F32)
        carry_out[part] = (
            jnp.where(line < row_start, mine, zero) + jnp.where(line < shift, theirs, zero)
        ).astype(BF16)
        object_out[part] = jnp.where(line >= row_start, mine, zero) + jnp.where(
            line >= shift, theirs, zero
        )

    @pl.when(has_upper)
    def _():
        send_carry.start()

    for index in range(CHAIN_PARTS):
        @pl.when(t < root)
        def _():
            down_to_lower(index).wait_recv()

            @pl.when(has_lower)
            def _():
                down_to_lower(index).start()

            down_to_sibling(index).start()

        @pl.when(t > root)
        def _():
            down_to_upper(index).wait_recv()

            @pl.when(has_upper)
            def _():
                down_to_upper(index).start()

            down_to_sibling(index).start()

        rows = part_rows(index)
        target = pl.ds(pl.multiple_of(r * half + index * chunk, chunk), chunk)
        probe_out[0, 0, target, :] = down[rows, :points].astype(F32)
        probe_out[0, 1, target, :] = down[rows, points:].astype(F32)

    for index in range(CHAIN_PARTS):
        down_to_sibling(index).wait()
        rows = part_rows(index)
        target = pl.ds(pl.multiple_of((1 - r) * half + index * chunk, chunk), chunk)
        probe_out[0, 0, target, :] = down_in[rows, :points].astype(F32)
        probe_out[0, 1, target, :] = down_in[rows, points:].astype(F32)

    @pl.when(has_lower)
    def _():
        send_carry.wait_recv()
        object_out[...] += carry_in[...].astype(F32)

    @pl.when(has_upper)
    def _():
        send_carry.wait_send()

    for index in range(CHAIN_PARTS):
        @pl.when(t < root)
        def _():
            up_to_upper(index).wait_send()

        @pl.when(t > root)
        def _():
            up_to_lower(index).wait_send()

        @pl.when((t <= root) & has_lower)
        def _():
            down_to_lower(index).wait_send()

        @pl.when((t >= root) & has_upper)
        def _():
            down_to_upper(index).wait_send()


def fused_local(tiles, object_tiles, probe_modes, measured, row_offset, col_offset):
    points = probe_modes.shape[-1]
    height, width = object_tiles.shape[1:]
    cosine, sine = (jnp.asarray(table) for table in cos_sin_tables(points))
    double, half = 2 * points, points // 2
    steps = points // POWER_ROWS
    vmem, smem = pl.BlockSpec(memory_space=pltpu.VMEM), pl.BlockSpec(memory_space=pltpu.SMEM)
    dma = pltpu.SemaphoreType.DMA
    scratch = [
        pltpu.VMEM((8, 2, height, width), BF16),
        pltpu.VMEM((8, 128), jnp.int32),
        pltpu.VMEM((8, 128), jnp.int32),
        pltpu.VMEM((points, points), BF16),
        pltpu.VMEM((points, points), BF16),
        pltpu.VMEM((double, double), BF16),
        pltpu.VMEM((double, double), BF16),
        pltpu.VMEM((double, double), BF16),
        pltpu.VMEM((double, double), BF16),
        pltpu.VMEM((2, points, points), BF16),
        pltpu.VMEM((2, points, points), BF16),
        pltpu.VMEM((double, points), BF16),
        pltpu.VMEM((points, double), BF16),
        pltpu.VMEM((points, double), F32),
        pltpu.VMEM((steps, POWER_ROWS, points), BF16),
        pltpu.VMEM((steps, POWER_ROWS, points), BF16),
        pltpu.VMEM((double, points), BF16),
        pltpu.VMEM((4, 2, height, points), BF16),
        pltpu.VMEM((2, 2, height, points), BF16),
        pltpu.VMEM((points, double), BF16),
        pltpu.VMEM((half, double), BF16),
        pltpu.VMEM((half, double), BF16),
        pltpu.VMEM((half, double), F32),
        pltpu.VMEM((half, double), BF16),
        pltpu.VMEM((half, double), BF16),
        pltpu.VMEM((half, double), BF16),
        pltpu.VMEM((half, double), BF16),
        pltpu.VMEM((half, double), BF16),
        pltpu.VMEM((2, height, width), BF16),
        pltpu.VMEM((2, height, width), BF16),
        pltpu.VMEM((2, height, width), BF16),
        pltpu.VMEM((2, height, width), BF16),
        pltpu.VMEM((2, height, width), BF16),
        dma((7, 2)), dma((7, 2)), dma, dma, dma((steps,)), dma((steps,)), dma((2,)), dma((2,)),
        dma, dma, dma((CHAIN_PARTS,)), dma((2, CHAIN_PARTS)), dma((2, CHAIN_PARTS)),
        dma((CHAIN_PARTS,)), dma((CHAIN_PARTS,)), dma((CHAIN_PARTS,)), dma, dma, dma, dma,
    ]
    return pl.pallas_call(
        functools.partial(fused_kernel, tiles),
        out_shape=(
            jax.ShapeDtypeStruct((2, height, width), F32),
            jax.ShapeDtypeStruct((1, 2, points, points), F32),
        ),
        in_specs=[smem, smem, vmem, vmem, vmem, vmem, vmem],
        out_specs=(vmem, vmem),
        scratch_shapes=scratch,
        compiler_params=pltpu.CompilerParams(
            collective_id=0, has_side_effects=True, vmem_limit_bytes=56 * 1024 * 1024
        ),
    )(row_offset, col_offset, object_tiles, probe_modes, cosine, sine, measured)


def solution(mesh):
    placed = (
        P(None, ("groups", "tile", "mode", "rep"), None),
        P(("groups", "mode"), None, None, None),
        P(("groups", "tile", "rep"), None, None),
        P(("groups", "tile", "rep")),
        P(("groups", "tile", "rep")),
    )
    if mesh.shape["mode"] == 2 and mesh.shape["rep"] == 2:
        body = functools.partial(fused_local, mesh.shape["tile"])
    else:
        body = local
    return jax.shard_map(
        body,
        mesh=mesh,
        in_specs=placed,
        out_specs=(
            P(None, ("groups", "tile", "mode", "rep"), None),
            P(("groups", "mode"), None, None, None),
        ),
        check_vma=False,
    )
```

```python
import functools
import math

import jax
import jax.numpy as jnp
import numpy as np
from jax import lax
from jax.experimental import pallas as pl
from jax.experimental.pallas import tpu as pltpu
from jax.sharding import PartitionSpec as P

PATCH = 512
F32, BF16 = jnp.float32, jnp.bfloat16
POWER_ROWS = 128
CHAIN_PARTS = 16
CHAIN_LAG = 6
GATHER_PARTS = 4

def passed_along(value, axis, steps):
    count = lax.axis_size(axis)
    initial, last = (max(0, -steps), min(count, count - steps))
    return lax.ppermute(value, axis, [(source, source + steps) for source in range(initial, last)])


def dft_tables(points):
    indices = jnp.arange(points, dtype=jnp.int32)
    products = indices[:, None] * indices[None, :] % points
    angles = products.astype(jnp.float32) * (2.0 * math.pi / points)
    norm_factor = 1.0 / math.sqrt(points)
    cos_table = (jnp.cos(angles) * norm_factor).astype(jnp.bfloat16)
    sin_table = (jnp.sin(angles) * norm_factor).astype(jnp.bfloat16)
    forward_left = jnp.concatenate(
        [jnp.concatenate([cos_table, sin_table], 1), jnp.concatenate([-sin_table, cos_table], 1)], 0
    )
    inverse_left = jnp.concatenate(
        [jnp.concatenate([cos_table, -sin_table], 1), jnp.concatenate([sin_table, cos_table], 1)], 0
    )
    return (cos_table, sin_table, forward_left, inverse_left)


def column_pass(left_matrix, stacked):
    points = stacked.shape[-1]
    product = jnp.dot(
        left_matrix, stacked.reshape(2 * points, points), preferred_element_type=jnp.float32
    )
    return product.reshape(2, points, points)


def row_pass(stacked, cos_table, sin_table, sign_flip):
    points = stacked.shape[-1]
    flattened = stacked.reshape(2 * points, points)
    with_cos = jnp.dot(flattened, cos_table, preferred_element_type=jnp.float32).reshape(
        2, points, points
    )
    with_sin = jnp.dot(flattened, sin_table, preferred_element_type=jnp.float32).reshape(
        2, points, points
    )
    real_part = with_cos[0] + sign_flip * with_sin[1]
    imag_part = with_cos[1] - sign_flip * with_sin[0]
    return jnp.stack([real_part, imag_part])


def forward_wave(exit_wave, tables):
    cos_table, sin_table, forward_left, inverse_left = tables
    middle = column_pass(forward_left, exit_wave).astype(jnp.bfloat16)
    return row_pass(middle, cos_table, sin_table, 1.0)


def inverse_wave(corrected, tables):
    cos_table, sin_table, forward_left, inverse_left = tables
    middle = column_pass(inverse_left, corrected).astype(jnp.bfloat16)
    return row_pass(middle, cos_table, sin_table, -1.0)


def complex_times(first, second):
    real_part = first[0] * second[0] - first[1] * second[1]
    imag_part = first[0] * second[1] + first[1] * second[0]
    return jnp.stack([real_part, imag_part])


def conj_times(first, second):
    real_part = first[0] * second[0] + first[1] * second[1]
    imag_part = first[0] * second[1] - first[1] * second[0]
    return jnp.stack([real_part, imag_part])


def local(object_tiles, probe_modes, measured, row_offset, col_offset):
    tables = dft_tables(PATCH)
    own_rows = lax.all_gather(object_tiles, ("mode", "rep"), axis=1, tiled=True)
    next_rows = passed_along(own_rows, "tile", -1)
    extended = jnp.concatenate([own_rows, next_rows], axis=1)
    tile_rows = own_rows.shape[1]
    obj_cols = extended.shape[2]
    zero_index = jnp.zeros((), jnp.int32)
    row_start = row_offset[0]
    col_start = col_offset[0]
    obj_patch = lax.dynamic_slice(
        extended, (zero_index, row_start, col_start), (2, PATCH, PATCH)
    ).astype(jnp.float32)
    probe_float = probe_modes[0].astype(jnp.float32)
    exit_wave = complex_times(probe_float, obj_patch).astype(jnp.bfloat16)
    spectra = forward_wave(exit_wave, tables)
    local_power = spectra[0] ** 2 + spectra[1] ** 2
    intensity = lax.psum(local_power.astype(jnp.bfloat16), "mode").astype(jnp.float32)
    factor = 1.0 - measured[0] / jnp.sqrt(jnp.maximum(intensity, 1.0))
    corrected = (spectra * factor).astype(jnp.bfloat16)
    back_wave = inverse_wave(corrected, tables)
    obj_term = conj_times(probe_float, back_wave).astype(jnp.bfloat16).astype(jnp.float32)
    extended_term = jnp.zeros((2, 2 * tile_rows, obj_cols), jnp.float32)
    extended_term = lax.dynamic_update_slice(
        extended_term, obj_term, (zero_index, row_start, col_start)
    )
    own_sum, next_sum = (
        lax.psum_scatter(
            extended_term[:, :tile_rows].astype(jnp.bfloat16),
            ("mode", "rep"),
            scatter_dimension=1,
            tiled=True,
        ).astype(jnp.float32),
        lax.psum_scatter(
            extended_term[:, tile_rows:].astype(jnp.bfloat16),
            ("mode", "rep"),
            scatter_dimension=1,
            tiled=True,
        ).astype(jnp.float32),
    )
    carried = passed_along(next_sum.astype(jnp.bfloat16), "tile", 1).astype(next_sum.dtype)
    object_grad = own_sum + carried
    probe_term = conj_times(obj_patch, back_wave)
    probe_grad = lax.psum(probe_term.astype(jnp.bfloat16), ("tile", "rep")).astype(jnp.float32)
    return (object_grad, probe_grad[None])


def cos_sin_tables(points):
    products = np.outer(np.arange(points), np.arange(points)) % points
    angles = products * (2.0 * math.pi / points)
    norm_factor = 1.0 / math.sqrt(points)
    return (
        (np.cos(angles) * norm_factor).astype(jnp.bfloat16),
        (np.sin(angles) * norm_factor).astype(jnp.bfloat16),
    )


def matmul(left, right):
    return jnp.dot(left, right, preferred_element_type=F32)


def rows_at(start, size):
    return pl.ds(pl.multiple_of(start, size), size)


def fused_kernel(
    tiles, row_ref, col_ref, obj, probe_hbm, cos_hbm, sin_hbm, measured_hbm, object_out, probe_out,
    probe, cos_ref, sin_ref, measured,
    ext, shift_out, shift_in, rotate, rotate_back, left_fwd, right_fwd, right_inv, left_inv,
    probe_rot, patch, wave, middle, spec, power, power_in, back_stack, term, term_in,
    probe_term, half_out, half_in, half_sum, up_left, up_right, up_out, down, down_in,
    placed_out, placed_mine, placed_in, carry_out, carry_in, own_sum,
    g_send, g_recv, s_send, s_recv, pw_send, pw_recv, t_send, t_recv, h_send, h_recv, load,
    up_send, up_recv, dn_send, dn_recv, sib_send, sib_recv, pl_send, pl_recv, c_send, c_recv,
):
    t, m, r = lax.axis_index("tile"), lax.axis_index("mode"), lax.axis_index("rep")
    sibling, partner = {"rep": 1 - r}, {"mode": 1 - m}
    lower, upper = {"tile": t - 1}, {"tile": t + 1}
    has_lower, has_upper = t > 0, t < tiles - 1
    height, width = obj.shape[1], obj.shape[2]
    points = probe.shape[-1]
    piece = 2 * height // GATHER_PARTS
    row_start, col_start = row_ref[0], col_ref[0]

    def copy(src, dst, send, recv, device):
        return pltpu.make_async_remote_copy(
            src_ref=src, dst_ref=dst, send_sem=send, recv_sem=recv,
            device_id=device, device_id_type=pl.DeviceIdType.MESH,
        )

    own_slot, other_slot = 2 * m + r, 2 * (1 - m) + r
    loads = [
        pltpu.make_async_copy(src, dst, load.at[index])
        for index, (src, dst) in enumerate(
            (
                (probe_hbm, probe), (cos_hbm, cos_ref), (sin_hbm, sin_ref),
                (measured_hbm, measured), (obj, ext.at[own_slot]),
            )
        )
    ]
    for one in loads:
        one.start()

    barrier = pltpu.get_barrier_semaphore()
    for device in (sibling, partner):
        pl.semaphore_signal(barrier, inc=1, device_id=device, device_id_type=pl.DeviceIdType.MESH)

    @pl.when(has_lower)
    def _():
        pl.semaphore_signal(barrier, inc=1, device_id=lower, device_id_type=pl.DeviceIdType.MESH)

    @pl.when(has_upper)
    def _():
        pl.semaphore_signal(barrier, inc=1, device_id=upper, device_id_type=pl.DeviceIdType.MESH)

    peers = 2 + has_lower.astype(jnp.int32) + has_upper.astype(jnp.int32)
    pl.semaphore_wait(barrier, peers)


    def lines(part):
        return part // (GATHER_PARTS // 2), pl.ds(part % (GATHER_PARTS // 2) * piece, piece)

    def gather(kind, part, src, slot, device):
        return copy(src, ext.at[slot, *lines(part)], g_send.at[kind, part], g_recv.at[kind, part], device)

    def block(slot, part):
        return ext.at[slot, *lines(part)]

    def to_sibling(part):
        return gather(0, part, obj.at[*lines(part)], own_slot, sibling)

    def to_partner(part):
        return gather(1, part, obj.at[*lines(part)], own_slot, partner)

    def to_lower(part):
        return gather(2, part, obj.at[*lines(part)], 4 + own_slot, lower)

    def relay_partner(part):
        return gather(3, part, block(other_slot, part), other_slot, sibling)

    def relay_upper(part):
        return gather(4, part, block(4 + own_slot, part), 4 + own_slot, sibling)

    def cross_partner(part):
        return gather(5, part, block(4 + own_slot, part), 4 + own_slot, partner)

    def cross_lower(part):
        return gather(5, part, block(other_slot, part), 4 + other_slot, lower)

    def relay_cross(part):
        return gather(6, part, block(4 + other_slot, part), 4 + other_slot, sibling)

    for part in range(GATHER_PARTS):
        to_partner(part).start()

        @pl.when(has_lower)
        def _():
            to_lower(part).start()

        to_sibling(part).start()
    shift_out[...] = jnp.full(shift_out.shape, row_start, jnp.int32)
    send_shift = copy(shift_out, shift_in, s_send, s_recv, sibling)
    send_shift.start()

    first = lax.broadcasted_iota(jnp.int32, (points, points), 0)
    second = lax.broadcasted_iota(jnp.int32, (points, points), 1)
    apart = first - second - row_start
    rotate[...] = jnp.where((apart == 0) | (apart == -points), 1.0, 0.0).astype(BF16)
    apart = second - first - row_start
    rotate_back[...] = jnp.where((apart == 0) | (apart == -points), 1.0, 0.0).astype(BF16)
    for one in loads[:3]:
        one.wait()
    cosine, sine = cos_ref[...], sin_ref[...]
    minus = -sine
    right_fwd[:points, :points] = cosine
    right_fwd[:points, points:] = minus
    right_fwd[points:, :points] = sine
    right_fwd[points:, points:] = cosine
    right_inv[:points, :points] = cosine
    right_inv[:points, points:] = sine
    right_inv[points:, :points] = minus
    right_inv[points:, points:] = cosine

    @pl.loop(0, 4)
    def _(step):
        rows = rows_at(step * 128, 128)
        low = rows_at(points + step * 128, 128)
        turn = rotate[rows, :]
        cos_rot = matmul(turn, cos_ref[...]).astype(BF16)
        sin_rot = matmul(turn, sin_ref[...]).astype(BF16)
        left_inv[rows, :points] = cos_rot
        left_inv[rows, points:] = -sin_rot
        left_inv[low, :points] = sin_rot
        left_inv[low, points:] = cos_rot
        cos_turn = matmul(cos_ref[rows, :], rotate_back[...]).astype(BF16)
        sin_turn = matmul(sin_ref[rows, :], rotate_back[...]).astype(BF16)
        left_fwd[rows, :points] = cos_turn
        left_fwd[rows, points:] = sin_turn
        left_fwd[low, :points] = -sin_turn
        left_fwd[low, points:] = cos_turn
        for part in range(2):
            probe_rot[part, rows, :] = matmul(turn, probe[0, part]).astype(BF16)

    for one in loads[3:]:
        one.wait()

    @pl.when(jnp.logical_not(has_upper))
    def _():
        ext[4:8] = jnp.zeros((4, 2, height, width), BF16)

    @pl.when(t == 0)
    def _():
        up_left[...] = jnp.zeros_like(up_left)

    @pl.when(t == tiles - 1)
    def _():
        up_right[...] = jnp.zeros_like(up_right)

    for part in range(GATHER_PARTS):
        gather(1, part, obj.at[*lines(part)], other_slot, partner).wait_recv()
        relay_partner(part).start()

        @pl.when((r == 1) & has_lower)
        def _():
            cross_lower(part).start()

        @pl.when(has_upper)
        def _():
            gather(2, part, obj.at[*lines(part)], 4 + own_slot, lower).wait_recv()
            relay_upper(part).start()

            @pl.when(r == 0)
            def _():
                cross_partner(part).start()

    for part in range(GATHER_PARTS):
        to_sibling(part).wait_recv()

        @pl.when(has_upper)
        def _():
            relay_upper(part).wait_recv()

    pick = lax.broadcasted_iota(jnp.int32, (width, points), 0) - lax.broadcasted_iota(
        jnp.int32, (width, points), 1
    )
    pick = jnp.where(pick == col_start, 1.0, 0.0).astype(BF16)

    def exit_rows(side):
        @pl.loop(0, 2)
        def _(index):
            step = 2 * side + index
            rows = rows_at(step * height, height)
            low = rows_at(points + step * height, height)
            line = lax.broadcasted_iota(jnp.int32, (height, width), 0) + step * height
            parts = []
            for part in range(2):
                chosen = jnp.where(
                    line >= row_start, ext[step, part].astype(F32), ext[4 + step, part].astype(F32)
                )
                parts.append(matmul(chosen.astype(BF16), pick))
                patch[part, rows, :] = parts[part].astype(BF16)
            obj_re, obj_im = parts
            prb_re, prb_im = (probe_rot[part, rows, :].astype(F32) for part in range(2))
            wave[rows, :] = (prb_re * obj_re - prb_im * obj_im).astype(BF16)
            wave[low, :] = (prb_re * obj_im + prb_im * obj_re).astype(BF16)

    def column_part(rows, side):
        near = rows_at(2 * side * height, 2 * height)
        far = rows_at(points + 2 * side * height, 2 * height)
        return matmul(left_fwd[rows, near], wave[near, :]) + matmul(left_fwd[rows, far], wave[far, :])

    exit_rows(m)

    @pl.loop(0, 2)
    def _(step):
        rows = rows_at(step * 256, 256)
        low = rows_at(points + step * 256, 256)
        spec[rows, :points] = column_part(rows, m)
        spec[rows, points:] = column_part(low, m)

    for part in range(GATHER_PARTS):
        @pl.when(has_upper)
        def _():
            gather(5, part, obj.at[*lines(part)], 4 + other_slot, partner).wait_recv()
            relay_cross(part).start()

    for part in range(GATHER_PARTS):
        relay_partner(part).wait_recv()

        @pl.when(has_upper)
        def _():
            relay_cross(part).wait_recv()

    exit_rows(1 - m)

    @pl.loop(0, 2)
    def _(step):
        rows = rows_at(step * 256, 256)
        low = rows_at(points + step * 256, 256)
        middle[rows, :points] = (spec[rows, :points] + column_part(rows, 1 - m)).astype(BF16)
        middle[rows, points:] = (spec[rows, points:] + column_part(low, 1 - m)).astype(BF16)

    def send_power(step):
        return copy(
            power.at[step], power_in.at[step], pw_send.at[step], pw_recv.at[step], partner
        )

    steps = points // POWER_ROWS

    @pl.loop(0, steps)
    def _(step):
        rows = rows_at(step * POWER_ROWS, POWER_ROWS)
        wide = matmul(middle[rows, :], right_fwd[...])
        spec[rows, :] = wide
        power[step] = (wide[:, :points] ** 2 + wide[:, points:] ** 2).astype(BF16)
        send_power(step).start()

    @pl.loop(0, steps)
    def _(step):
        rows = rows_at(step * POWER_ROWS, POWER_ROWS)
        low = rows_at(points + step * POWER_ROWS, POWER_ROWS)
        send_power(step).wait()
        spec_re, spec_im = spec[rows, :points], spec[rows, points:]
        intensity = spec_re**2 + spec_im**2 + power_in[step].astype(F32)
        factor = 1.0 - measured[0, rows, :] / jnp.sqrt(jnp.maximum(intensity, 1.0))
        corrected = jnp.concatenate(
            [(spec_re * factor).astype(BF16), (spec_im * factor).astype(BF16)], 1
        )
        turned = matmul(corrected, right_inv[...]).astype(BF16)
        back_stack[rows, :] = turned[:, :points]
        back_stack[low, :] = turned[:, points:]

    for part in range(GATHER_PARTS):
        to_sibling(part).wait_send()
        to_partner(part).wait_send()
        relay_partner(part).wait_send()

        @pl.when(has_lower)
        def _():
            to_lower(part).wait_send()

        @pl.when((r == 1) & has_lower)
        def _():
            cross_lower(part).wait_send()

        @pl.when(has_upper)
        def _():
            relay_upper(part).wait_send()
            relay_cross(part).wait_send()

        @pl.when((r == 0) & has_upper)
        def _():
            cross_partner(part).wait_send()

    def send_term(which, part):
        return copy(
            term.at[2 * (1 - m) + which, part], term_in.at[which, part],
            t_send.at[which, part], t_recv.at[which, part], partner,
        )

    @pl.loop(0, 4)
    def _(step):
        slot = (step + 2 * (1 - m)) % 4
        rows = rows_at(slot * height, height)
        low = rows_at(points + slot * height, height)
        back_re = matmul(left_inv[rows, :], back_stack[...])
        back_im = matmul(left_inv[low, :], back_stack[...])
        prb_re, prb_im = (probe_rot[part, rows, :].astype(F32) for part in range(2))
        term[slot, 0] = (prb_re * back_re + prb_im * back_im).astype(BF16)
        term[slot, 1] = (prb_re * back_im - prb_im * back_re).astype(BF16)

        @pl.when(step == 1)
        def _():
            for part in range(2):
                send_term(1 - r, part).start()
                send_term(r, part).start()

        obj_re, obj_im = (patch[part, rows, :].astype(F32) for part in range(2))
        probe_term[rows, :points] = (obj_re * back_re + obj_im * back_im).astype(BF16)
        probe_term[rows, points:] = (obj_re * back_im - obj_im * back_re).astype(BF16)

    half = points // 2
    chunk = half // CHAIN_PARTS
    half_out[...] = matmul(rotate_back[rows_at((1 - r) * half, half), :], probe_term[...]).astype(BF16)
    send_half = copy(half_out, half_in, h_send, h_recv, sibling)
    send_half.start()
    half_sum[...] = matmul(rotate_back[rows_at(r * half, half), :], probe_term[...])
    send_half.wait()
    half_sum[...] += half_in[...].astype(F32)
    root = tiles // 2

    def part_rows(index):
        return pl.ds(pl.multiple_of(index * chunk, chunk), chunk)

    def up_to_upper(index):
        rows = part_rows(index)
        return copy(up_out.at[rows], up_left.at[rows], up_send.at[index], up_recv.at[0, index], upper)

    def up_to_lower(index):
        rows = part_rows(index)
        return copy(up_out.at[rows], up_right.at[rows], up_send.at[index], up_recv.at[1, index], lower)

    def down_to_upper(index):
        rows = part_rows(index)
        return copy(down.at[rows], down.at[rows], dn_send.at[0, index], dn_recv.at[index], upper)

    def down_to_lower(index):
        rows = part_rows(index)
        return copy(down.at[rows], down.at[rows], dn_send.at[1, index], dn_recv.at[index], lower)

    def down_to_sibling(index):
        rows = part_rows(index)
        return copy(down.at[rows], down_in.at[rows], sib_send.at[index], sib_recv.at[index], sibling)

    def chain_up(index):
        rows = part_rows(index)

        @pl.when((t <= root) & has_lower)
        def _():
            up_to_upper(index).wait_recv()

        @pl.when((t >= root) & has_upper)
        def _():
            up_to_lower(index).wait_recv()

        @pl.when(t < root)
        def _():
            up_out[rows] = (half_sum[rows] + up_left[rows].astype(F32)).astype(BF16)
            up_to_upper(index).start()

        @pl.when(t > root)
        def _():
            up_out[rows] = (half_sum[rows] + up_right[rows].astype(F32)).astype(BF16)
            up_to_lower(index).start()

        @pl.when(t == root)
        def _():
            down[rows] = (
                half_sum[rows] + up_left[rows].astype(F32) + up_right[rows].astype(F32)
            ).astype(BF16)

            @pl.when(has_lower)
            def _():
                down_to_lower(index).start()

            @pl.when(has_upper)
            def _():
                down_to_upper(index).start()

    def chain_down(index):
        @pl.when(t < root)
        def _():
            down_to_lower(index).wait_recv()

            @pl.when(has_lower)
            def _():
                down_to_lower(index).start()

        @pl.when(t > root)
        def _():
            down_to_upper(index).wait_recv()

            @pl.when(has_upper)
            def _():
                down_to_upper(index).start()

        down_to_sibling(index).start()
        target = pl.ds(pl.multiple_of(r * half + index * chunk, chunk), chunk)
        rows = part_rows(index)
        probe_out[0, 0, target, :] = down[rows, :points]
        probe_out[0, 1, target, :] = down[rows, points:]

    def chain(start, stop):
        @pl.loop(start, stop)
        def _(index):
            chain_up(index)
            chain_down(index - CHAIN_LAG)

    place = lax.broadcasted_iota(jnp.int32, (points, width), 1) - lax.broadcasted_iota(
        jnp.int32, (points, width), 0
    )
    place = jnp.where(place == col_start, 1.0, 0.0).astype(BF16)
    line = lax.broadcasted_iota(jnp.int32, (height, width), 0) + own_slot * height

    def send_placed(part):
        return copy(
            placed_out.at[part], placed_in.at[part], pl_send.at[part], pl_recv.at[part], sibling
        )

    def send_carry(part):
        return copy(carry_out.at[part], carry_in.at[part], c_send.at[part], c_recv.at[part], upper)

    def object_part(part):
        for which, target in ((1 - r, placed_out), (r, placed_mine)):
            send_term(which, part).wait()
            total = term[2 * m + which, part].astype(F32) + term_in[which, part].astype(F32)
            target[part] = matmul(total.astype(BF16), place).astype(BF16)
            if target is placed_out:
                send_placed(part).start()
        send_placed(part).wait()
        shift = shift_in[0:1, :]
        shift = jnp.broadcast_to(jnp.concatenate([shift] * (width // 128), 1), (height, width))
        zero = jnp.zeros((height, width), F32)
        mine, theirs = placed_mine[part].astype(F32), placed_in[part].astype(F32)
        carry_out[part] = (
            jnp.where(line < row_start, mine, zero) + jnp.where(line < shift, theirs, zero)
        ).astype(BF16)

        @pl.when(has_upper)
        def _():
            send_carry(part).start()

        own_sum[part] = jnp.where(line >= row_start, mine, zero) + jnp.where(
            line >= shift, theirs, zero
        )

    @pl.loop(0, CHAIN_LAG)
    def _(index):
        chain_up(index)

    chain(CHAIN_LAG, 8)
    send_shift.wait()
    object_part(0)
    chain(8, 13)
    object_part(1)
    chain(13, CHAIN_PARTS)

    @pl.loop(CHAIN_PARTS - CHAIN_LAG, CHAIN_PARTS)
    def _(index):
        chain_down(index)

    @pl.loop(0, CHAIN_PARTS)
    def _(index):
        down_to_sibling(index).wait()

        @pl.when(t < root)
        def _():
            up_to_upper(index).wait_send()

        @pl.when(t > root)
        def _():
            up_to_lower(index).wait_send()

        @pl.when((t <= root) & has_lower)
        def _():
            down_to_lower(index).wait_send()

        @pl.when((t >= root) & has_upper)
        def _():
            down_to_upper(index).wait_send()

    target = rows_at((1 - r) * half, half)
    probe_out[0, 0, target, :] = down_in[:, :points]
    probe_out[0, 1, target, :] = down_in[:, points:]

    for part in range(2):
        @pl.when(has_lower)
        def _():
            send_carry(part).wait_recv()
            object_out[part] = (own_sum[part] + carry_in[part].astype(F32)).astype(BF16)

        @pl.when(jnp.logical_not(has_lower))
        def _():
            object_out[part] = own_sum[part].astype(BF16)

        @pl.when(has_upper)
        def _():
            send_carry(part).wait_send()


def fused_local(tiles, object_tiles, probe_modes, measured, row_offset, col_offset):
    points = probe_modes.shape[-1]
    height, width = object_tiles.shape[1:]
    cosine, sine = (jnp.asarray(table) for table in cos_sin_tables(points))
    double, half = 2 * points, points // 2
    steps = points // POWER_ROWS
    vmem, smem = pl.BlockSpec(memory_space=pltpu.VMEM), pl.BlockSpec(memory_space=pltpu.SMEM)
    dma = pltpu.SemaphoreType.DMA
    scratch = [
        pltpu.VMEM(probe_modes.shape, BF16),
        pltpu.VMEM((points, points), BF16),
        pltpu.VMEM((points, points), BF16),
        pltpu.VMEM(measured.shape, F32),
        pltpu.VMEM((8, 2, height, width), BF16),
        pltpu.VMEM((8, 128), jnp.int32),
        pltpu.VMEM((8, 128), jnp.int32),
        pltpu.VMEM((points, points), BF16),
        pltpu.VMEM((points, points), BF16),
        pltpu.VMEM((double, double), BF16),
        pltpu.VMEM((double, double), BF16),
        pltpu.VMEM((double, double), BF16),
        pltpu.VMEM((double, double), BF16),
        pltpu.VMEM((2, points, points), BF16),
        pltpu.VMEM((2, points, points), BF16),
        pltpu.VMEM((double, points), BF16),
        pltpu.VMEM((points, double), BF16),
        pltpu.VMEM((points, double), F32),
        pltpu.VMEM((steps, POWER_ROWS, points), BF16),
        pltpu.VMEM((steps, POWER_ROWS, points), BF16),
        pltpu.VMEM((double, points), BF16),
        pltpu.VMEM((4, 2, height, points), BF16),
        pltpu.VMEM((2, 2, height, points), BF16),
        pltpu.VMEM((points, double), BF16),
        pltpu.VMEM((half, double), BF16),
        pltpu.VMEM((half, double), BF16),
        pltpu.VMEM((half, double), F32),
        pltpu.VMEM((half, double), BF16),
        pltpu.VMEM((half, double), BF16),
        pltpu.VMEM((half, double), BF16),
        pltpu.VMEM((half, double), BF16),
        pltpu.VMEM((half, double), BF16),
        pltpu.VMEM((2, height, width), BF16),
        pltpu.VMEM((2, height, width), BF16),
        pltpu.VMEM((2, height, width), BF16),
        pltpu.VMEM((2, height, width), BF16),
        pltpu.VMEM((2, height, width), BF16),
        pltpu.VMEM((2, height, width), F32),
        dma((7, GATHER_PARTS)), dma((7, GATHER_PARTS)), dma, dma, dma((steps,)), dma((steps,)), dma((2, 2)), dma((2, 2)),
        dma, dma, dma((5,)), dma((CHAIN_PARTS,)), dma((2, CHAIN_PARTS)), dma((2, CHAIN_PARTS)),
        dma((CHAIN_PARTS,)), dma((CHAIN_PARTS,)), dma((CHAIN_PARTS,)), dma((2,)), dma((2,)), dma((2,)), dma((2,)),
    ]
    object_grad, probe_grad = pl.pallas_call(
        functools.partial(fused_kernel, tiles),
        out_shape=(
            jax.ShapeDtypeStruct((2, height, width), BF16),
            jax.ShapeDtypeStruct((1, 2, points, points), BF16),
        ),
        in_specs=[smem, smem] + [pl.BlockSpec(memory_space=pl.ANY)] * 5,
        out_specs=(vmem, vmem),
        scratch_shapes=scratch,
        compiler_params=pltpu.CompilerParams(
            collective_id=0, has_side_effects=True, vmem_limit_bytes=56 * 1024 * 1024
        ),
    )(row_offset, col_offset, object_tiles, probe_modes, cosine, sine, measured)
    return object_grad.astype(F32), probe_grad.astype(F32)


def solution(mesh):
    placed = (
        P(None, ("groups", "tile", "mode", "rep"), None),
        P(("groups", "mode"), None, None, None),
        P(("groups", "tile", "rep"), None, None),
        P(("groups", "tile", "rep")),
        P(("groups", "tile", "rep")),
    )
    if mesh.shape["mode"] == 2 and mesh.shape["rep"] == 2:
        body = functools.partial(fused_local, mesh.shape["tile"])
    else:
        body = local
    return jax.shard_map(
        body,
        mesh=mesh,
        in_specs=placed,
        out_specs=(
            P(None, ("groups", "tile", "mode", "rep"), None),
            P(("groups", "mode"), None, None, None),
        ),
        check_vma=False,
    )
```

```python
import functools
import math

import jax
import jax.numpy as jnp
import numpy as np
from jax import lax
from jax.experimental import pallas as pl
from jax.experimental.pallas import tpu as pltpu
from jax.sharding import PartitionSpec as P

PATCH = 512
F32, BF16 = jnp.float32, jnp.bfloat16
POWER_ROWS = 128
CHAIN_PARTS = 16
CHAIN_LAG = 7
GATHER_PARTS = 4

def passed_along(value, axis, steps):
    count = lax.axis_size(axis)
    initial, last = (max(0, -steps), min(count, count - steps))
    return lax.ppermute(value, axis, [(source, source + steps) for source in range(initial, last)])


def dft_tables(points):
    indices = jnp.arange(points, dtype=jnp.int32)
    products = indices[:, None] * indices[None, :] % points
    angles = products.astype(jnp.float32) * (2.0 * math.pi / points)
    norm_factor = 1.0 / math.sqrt(points)
    cos_table = (jnp.cos(angles) * norm_factor).astype(jnp.bfloat16)
    sin_table = (jnp.sin(angles) * norm_factor).astype(jnp.bfloat16)
    forward_left = jnp.concatenate(
        [jnp.concatenate([cos_table, sin_table], 1), jnp.concatenate([-sin_table, cos_table], 1)], 0
    )
    inverse_left = jnp.concatenate(
        [jnp.concatenate([cos_table, -sin_table], 1), jnp.concatenate([sin_table, cos_table], 1)], 0
    )
    return (cos_table, sin_table, forward_left, inverse_left)


def column_pass(left_matrix, stacked):
    points = stacked.shape[-1]
    product = jnp.dot(
        left_matrix, stacked.reshape(2 * points, points), preferred_element_type=jnp.float32
    )
    return product.reshape(2, points, points)


def row_pass(stacked, cos_table, sin_table, sign_flip):
    points = stacked.shape[-1]
    flattened = stacked.reshape(2 * points, points)
    with_cos = jnp.dot(flattened, cos_table, preferred_element_type=jnp.float32).reshape(
        2, points, points
    )
    with_sin = jnp.dot(flattened, sin_table, preferred_element_type=jnp.float32).reshape(
        2, points, points
    )
    real_part = with_cos[0] + sign_flip * with_sin[1]
    imag_part = with_cos[1] - sign_flip * with_sin[0]
    return jnp.stack([real_part, imag_part])


def forward_wave(exit_wave, tables):
    cos_table, sin_table, forward_left, inverse_left = tables
    middle = column_pass(forward_left, exit_wave).astype(jnp.bfloat16)
    return row_pass(middle, cos_table, sin_table, 1.0)


def inverse_wave(corrected, tables):
    cos_table, sin_table, forward_left, inverse_left = tables
    middle = column_pass(inverse_left, corrected).astype(jnp.bfloat16)
    return row_pass(middle, cos_table, sin_table, -1.0)


def complex_times(first, second):
    real_part = first[0] * second[0] - first[1] * second[1]
    imag_part = first[0] * second[1] + first[1] * second[0]
    return jnp.stack([real_part, imag_part])


def conj_times(first, second):
    real_part = first[0] * second[0] + first[1] * second[1]
    imag_part = first[0] * second[1] - first[1] * second[0]
    return jnp.stack([real_part, imag_part])


def local(object_tiles, probe_modes, measured, row_offset, col_offset):
    tables = dft_tables(PATCH)
    own_rows = lax.all_gather(object_tiles, ("mode", "rep"), axis=1, tiled=True)
    next_rows = passed_along(own_rows, "tile", -1)
    extended = jnp.concatenate([own_rows, next_rows], axis=1)
    tile_rows = own_rows.shape[1]
    obj_cols = extended.shape[2]
    zero_index = jnp.zeros((), jnp.int32)
    row_start = row_offset[0]
    col_start = col_offset[0]
    obj_patch = lax.dynamic_slice(
        extended, (zero_index, row_start, col_start), (2, PATCH, PATCH)
    ).astype(jnp.float32)
    probe_float = probe_modes[0].astype(jnp.float32)
    exit_wave = complex_times(probe_float, obj_patch).astype(jnp.bfloat16)
    spectra = forward_wave(exit_wave, tables)
    local_power = spectra[0] ** 2 + spectra[1] ** 2
    intensity = lax.psum(local_power.astype(jnp.bfloat16), "mode").astype(jnp.float32)
    factor = 1.0 - measured[0] / jnp.sqrt(jnp.maximum(intensity, 1.0))
    corrected = (spectra * factor).astype(jnp.bfloat16)
    back_wave = inverse_wave(corrected, tables)
    obj_term = conj_times(probe_float, back_wave).astype(jnp.bfloat16).astype(jnp.float32)
    extended_term = jnp.zeros((2, 2 * tile_rows, obj_cols), jnp.float32)
    extended_term = lax.dynamic_update_slice(
        extended_term, obj_term, (zero_index, row_start, col_start)
    )
    own_sum, next_sum = (
        lax.psum_scatter(
            extended_term[:, :tile_rows].astype(jnp.bfloat16),
            ("mode", "rep"),
            scatter_dimension=1,
            tiled=True,
        ).astype(jnp.float32),
        lax.psum_scatter(
            extended_term[:, tile_rows:].astype(jnp.bfloat16),
            ("mode", "rep"),
            scatter_dimension=1,
            tiled=True,
        ).astype(jnp.float32),
    )
    carried = passed_along(next_sum.astype(jnp.bfloat16), "tile", 1).astype(next_sum.dtype)
    object_grad = own_sum + carried
    probe_term = conj_times(obj_patch, back_wave)
    probe_grad = lax.psum(probe_term.astype(jnp.bfloat16), ("tile", "rep")).astype(jnp.float32)
    return (object_grad, probe_grad[None])


def cos_sin_tables(points):
    products = np.outer(np.arange(points), np.arange(points)) % points
    angles = products * (2.0 * math.pi / points)
    norm_factor = 1.0 / math.sqrt(points)
    return (
        (np.cos(angles) * norm_factor).astype(jnp.bfloat16),
        (np.sin(angles) * norm_factor).astype(jnp.bfloat16),
    )


def matmul(left, right):
    return jnp.dot(left, right, preferred_element_type=F32)


def rows_at(start, size):
    return pl.ds(pl.multiple_of(start, size), size)


def fused_kernel(
    tiles, row_ref, col_ref, obj, probe_hbm, cos_hbm, sin_hbm, measured_hbm, object_out, probe_out,
    probe, cos_ref, sin_ref, measured,
    ext, shift_out, shift_in, rotate, rotate_back, left_fwd, right_fwd, right_inv, left_inv,
    probe_rot, patch, wave, middle, spec, power, power_in, back_stack, term, term_in,
    probe_term, half_out, half_in, half_sum, up_left, up_right, up_out, down, down_in,
    placed_out, placed_mine, placed_in, carry_out, carry_in, own_sum,
    g_send, g_recv, s_send, s_recv, pw_send, pw_recv, t_send, t_recv, h_send, h_recv, load,
    up_send, up_recv, dn_send, dn_recv, sib_send, sib_recv, pl_send, pl_recv, c_send, c_recv,
):
    t, m, r = lax.axis_index("tile"), lax.axis_index("mode"), lax.axis_index("rep")
    sibling, partner = {"rep": 1 - r}, {"mode": 1 - m}
    lower, upper = {"tile": t - 1}, {"tile": t + 1}
    has_lower, has_upper = t > 0, t < tiles - 1
    height, width = obj.shape[1], obj.shape[2]
    points = probe.shape[-1]
    piece = 2 * height // GATHER_PARTS
    row_start, col_start = row_ref[0], col_ref[0]

    def copy(src, dst, send, recv, device):
        return pltpu.make_async_remote_copy(
            src_ref=src, dst_ref=dst, send_sem=send, recv_sem=recv,
            device_id=device, device_id_type=pl.DeviceIdType.MESH,
        )

    own_slot, other_slot = 2 * m + r, 2 * (1 - m) + r
    loads = [
        pltpu.make_async_copy(src, dst, load.at[index])
        for index, (src, dst) in enumerate(
            (
                (probe_hbm, probe), (cos_hbm, cos_ref), (sin_hbm, sin_ref),
                (measured_hbm, measured), (obj, ext.at[own_slot]),
            )
        )
    ]
    for one in loads:
        one.start()

    barrier = pltpu.get_barrier_semaphore()
    for device in (sibling, partner):
        pl.semaphore_signal(barrier, inc=1, device_id=device, device_id_type=pl.DeviceIdType.MESH)

    @pl.when(has_lower)
    def _():
        pl.semaphore_signal(barrier, inc=1, device_id=lower, device_id_type=pl.DeviceIdType.MESH)

    @pl.when(has_upper)
    def _():
        pl.semaphore_signal(barrier, inc=1, device_id=upper, device_id_type=pl.DeviceIdType.MESH)

    peers = 2 + has_lower.astype(jnp.int32) + has_upper.astype(jnp.int32)
    pl.semaphore_wait(barrier, peers)


    def lines(part):
        return part // (GATHER_PARTS // 2), pl.ds(part % (GATHER_PARTS // 2) * piece, piece)

    def gather(kind, part, src, slot, device):
        return copy(src, ext.at[slot, *lines(part)], g_send.at[kind, part], g_recv.at[kind, part], device)

    def block(slot, part):
        return ext.at[slot, *lines(part)]

    def to_sibling(part):
        return gather(0, part, obj.at[*lines(part)], own_slot, sibling)

    def to_partner(part):
        return gather(1, part, obj.at[*lines(part)], own_slot, partner)

    def to_lower(part):
        return gather(2, part, obj.at[*lines(part)], 4 + own_slot, lower)

    def relay_partner(part):
        return gather(3, part, block(other_slot, part), other_slot, sibling)

    def relay_upper(part):
        return gather(4, part, block(4 + own_slot, part), 4 + own_slot, sibling)

    def cross_partner(part):
        return gather(5, part, block(4 + own_slot, part), 4 + own_slot, partner)

    def cross_lower(part):
        return gather(5, part, block(other_slot, part), 4 + other_slot, lower)

    def relay_cross(part):
        return gather(6, part, block(4 + other_slot, part), 4 + other_slot, sibling)

    for part in range(GATHER_PARTS):
        to_partner(part).start()

        @pl.when(has_lower)
        def _():
            to_lower(part).start()

        to_sibling(part).start()
    shift_out[...] = jnp.full(shift_out.shape, row_start, jnp.int32)
    send_shift = copy(shift_out, shift_in, s_send, s_recv, sibling)
    send_shift.start()

    first = lax.broadcasted_iota(jnp.int32, (points, points), 0)
    second = lax.broadcasted_iota(jnp.int32, (points, points), 1)
    apart = first - second - row_start
    rotate[...] = jnp.where((apart == 0) | (apart == -points), 1.0, 0.0).astype(BF16)
    apart = second - first - row_start
    rotate_back[...] = jnp.where((apart == 0) | (apart == -points), 1.0, 0.0).astype(BF16)
    for one in loads[:3]:
        one.wait()
    cosine, sine = cos_ref[...], sin_ref[...]
    minus = -sine
    right_fwd[:points, :points] = cosine
    right_fwd[:points, points:] = minus
    right_fwd[points:, :points] = sine
    right_fwd[points:, points:] = cosine
    right_inv[:points, :points] = cosine
    right_inv[:points, points:] = sine
    right_inv[points:, :points] = minus
    right_inv[points:, points:] = cosine

    @pl.loop(0, 4)
    def _(step):
        rows = rows_at(step * 128, 128)
        low = rows_at(points + step * 128, 128)
        turn = rotate[rows, :]
        cos_rot = matmul(turn, cos_ref[...]).astype(BF16)
        sin_rot = matmul(turn, sin_ref[...]).astype(BF16)
        left_inv[rows, :points] = cos_rot
        left_inv[rows, points:] = -sin_rot
        left_inv[low, :points] = sin_rot
        left_inv[low, points:] = cos_rot
        cos_turn = matmul(cos_ref[rows, :], rotate_back[...]).astype(BF16)
        sin_turn = matmul(sin_ref[rows, :], rotate_back[...]).astype(BF16)
        left_fwd[rows, :points] = cos_turn
        left_fwd[rows, points:] = sin_turn
        left_fwd[low, :points] = -sin_turn
        left_fwd[low, points:] = cos_turn
        for part in range(2):
            probe_rot[part, rows, :] = matmul(turn, probe[0, part]).astype(BF16)

    for one in loads[3:]:
        one.wait()

    @pl.when(jnp.logical_not(has_upper))
    def _():
        ext[4:8] = jnp.zeros((4, 2, height, width), BF16)

    @pl.when(t == 0)
    def _():
        up_left[...] = jnp.zeros_like(up_left)

    @pl.when(t == tiles - 1)
    def _():
        up_right[...] = jnp.zeros_like(up_right)

    for part in range(GATHER_PARTS):
        gather(1, part, obj.at[*lines(part)], other_slot, partner).wait_recv()
        relay_partner(part).start()

        @pl.when((r == 1) & has_lower)
        def _():
            cross_lower(part).start()

        @pl.when(has_upper)
        def _():
            gather(2, part, obj.at[*lines(part)], 4 + own_slot, lower).wait_recv()
            relay_upper(part).start()

            @pl.when(r == 0)
            def _():
                cross_partner(part).start()

    for part in range(GATHER_PARTS):
        to_sibling(part).wait_recv()

        @pl.when(has_upper)
        def _():
            relay_upper(part).wait_recv()

    pick = lax.broadcasted_iota(jnp.int32, (width, points), 0) - lax.broadcasted_iota(
        jnp.int32, (width, points), 1
    )
    pick = jnp.where(pick == col_start, 1.0, 0.0).astype(BF16)

    def exit_rows(side):
        @pl.loop(0, 2)
        def _(index):
            step = 2 * side + index
            rows = rows_at(step * height, height)
            low = rows_at(points + step * height, height)
            line = lax.broadcasted_iota(jnp.int32, (height, width), 0) + step * height
            parts = []
            for part in range(2):
                chosen = jnp.where(
                    line >= row_start, ext[step, part].astype(F32), ext[4 + step, part].astype(F32)
                )
                parts.append(matmul(chosen.astype(BF16), pick))
                patch[part, rows, :] = parts[part].astype(BF16)
            obj_re, obj_im = parts
            prb_re, prb_im = (probe_rot[part, rows, :].astype(F32) for part in range(2))
            wave[rows, :] = (prb_re * obj_re - prb_im * obj_im).astype(BF16)
            wave[low, :] = (prb_re * obj_im + prb_im * obj_re).astype(BF16)

    def column_part(rows, side):
        near = rows_at(2 * side * height, 2 * height)
        far = rows_at(points + 2 * side * height, 2 * height)
        return matmul(left_fwd[rows, near], wave[near, :]) + matmul(left_fwd[rows, far], wave[far, :])

    exit_rows(m)

    @pl.loop(0, 2)
    def _(step):
        rows = rows_at(step * 256, 256)
        low = rows_at(points + step * 256, 256)
        spec[rows, :points] = column_part(rows, m)
        spec[rows, points:] = column_part(low, m)

    for part in range(GATHER_PARTS):
        @pl.when(has_upper)
        def _():
            gather(5, part, obj.at[*lines(part)], 4 + other_slot, partner).wait_recv()
            relay_cross(part).start()

    for part in range(GATHER_PARTS):
        relay_partner(part).wait_recv()

        @pl.when(has_upper)
        def _():
            relay_cross(part).wait_recv()

    exit_rows(1 - m)

    @pl.loop(0, 2)
    def _(step):
        rows = rows_at(step * 256, 256)
        low = rows_at(points + step * 256, 256)
        middle[rows, :points] = (spec[rows, :points] + column_part(rows, 1 - m)).astype(BF16)
        middle[rows, points:] = (spec[rows, points:] + column_part(low, 1 - m)).astype(BF16)

    def send_power(step):
        return copy(
            power.at[step], power_in.at[step], pw_send.at[step], pw_recv.at[step], partner
        )

    steps = points // POWER_ROWS

    @pl.loop(0, steps)
    def _(step):
        rows = rows_at(step * POWER_ROWS, POWER_ROWS)
        wide = matmul(middle[rows, :], right_fwd[...])
        spec[rows, :] = wide
        power[step] = (wide[:, :points] ** 2 + wide[:, points:] ** 2).astype(BF16)
        send_power(step).start()

    @pl.loop(0, steps)
    def _(step):
        rows = rows_at(step * POWER_ROWS, POWER_ROWS)
        low = rows_at(points + step * POWER_ROWS, POWER_ROWS)
        send_power(step).wait()
        spec_re, spec_im = spec[rows, :points], spec[rows, points:]
        intensity = spec_re**2 + spec_im**2 + power_in[step].astype(F32)
        factor = 1.0 - measured[0, rows, :] / jnp.sqrt(jnp.maximum(intensity, 1.0))
        corrected = jnp.concatenate(
            [(spec_re * factor).astype(BF16), (spec_im * factor).astype(BF16)], 1
        )
        turned = matmul(corrected, right_inv[...]).astype(BF16)
        back_stack[rows, :] = turned[:, :points]
        back_stack[low, :] = turned[:, points:]

    for part in range(GATHER_PARTS):
        to_sibling(part).wait_send()
        to_partner(part).wait_send()
        relay_partner(part).wait_send()

        @pl.when(has_lower)
        def _():
            to_lower(part).wait_send()

        @pl.when((r == 1) & has_lower)
        def _():
            cross_lower(part).wait_send()

        @pl.when(has_upper)
        def _():
            relay_upper(part).wait_send()
            relay_cross(part).wait_send()

        @pl.when((r == 0) & has_upper)
        def _():
            cross_partner(part).wait_send()

    def send_term(which, part):
        return copy(
            term.at[2 * (1 - m) + which, part], term_in.at[which, part],
            t_send.at[which, part], t_recv.at[which, part], partner,
        )

    @pl.loop(0, 4)
    def _(step):
        slot = (step + 2 * (1 - m)) % 4
        rows = rows_at(slot * height, height)
        low = rows_at(points + slot * height, height)
        back_re = matmul(left_inv[rows, :], back_stack[...])
        back_im = matmul(left_inv[low, :], back_stack[...])
        prb_re, prb_im = (probe_rot[part, rows, :].astype(F32) for part in range(2))
        term[slot, 0] = (prb_re * back_re + prb_im * back_im).astype(BF16)
        term[slot, 1] = (prb_re * back_im - prb_im * back_re).astype(BF16)

        @pl.when(step == 1)
        def _():
            for part in range(2):
                send_term(1 - r, part).start()
                send_term(r, part).start()

        obj_re, obj_im = (patch[part, rows, :].astype(F32) for part in range(2))
        probe_term[rows, :points] = (obj_re * back_re + obj_im * back_im).astype(BF16)
        probe_term[rows, points:] = (obj_re * back_im - obj_im * back_re).astype(BF16)

    half = points // 2
    chunk = half // CHAIN_PARTS
    half_out[...] = matmul(rotate_back[rows_at((1 - r) * half, half), :], probe_term[...]).astype(BF16)
    send_half = copy(half_out, half_in, h_send, h_recv, sibling)
    send_half.start()
    half_sum[...] = matmul(rotate_back[rows_at(r * half, half), :], probe_term[...])
    send_half.wait()
    half_sum[...] += half_in[...].astype(F32)
    root = tiles // 2

    def part_rows(index):
        return pl.ds(pl.multiple_of(index * chunk, chunk), chunk)

    def up_to_upper(index):
        rows = part_rows(index)
        return copy(up_out.at[rows], up_left.at[rows], up_send.at[index], up_recv.at[0, index], upper)

    def up_to_lower(index):
        rows = part_rows(index)
        return copy(up_out.at[rows], up_right.at[rows], up_send.at[index], up_recv.at[1, index], lower)

    def down_to_upper(index):
        rows = part_rows(index)
        return copy(down.at[rows], down.at[rows], dn_send.at[0, index], dn_recv.at[index], upper)

    def down_to_lower(index):
        rows = part_rows(index)
        return copy(down.at[rows], down.at[rows], dn_send.at[1, index], dn_recv.at[index], lower)

    def down_to_sibling(index):
        rows = part_rows(index)
        return copy(down.at[rows], down_in.at[rows], sib_send.at[index], sib_recv.at[index], sibling)

    def chain_up(index):
        rows = part_rows(index)

        @pl.when((t <= root) & has_lower)
        def _():
            up_to_upper(index).wait_recv()

        @pl.when((t >= root) & has_upper)
        def _():
            up_to_lower(index).wait_recv()

        @pl.when(t < root)
        def _():
            up_out[rows] = (half_sum[rows] + up_left[rows].astype(F32)).astype(BF16)
            up_to_upper(index).start()

        @pl.when(t > root)
        def _():
            up_out[rows] = (half_sum[rows] + up_right[rows].astype(F32)).astype(BF16)
            up_to_lower(index).start()

        @pl.when(t == root)
        def _():
            down[rows] = (
                half_sum[rows] + up_left[rows].astype(F32) + up_right[rows].astype(F32)
            ).astype(BF16)

            @pl.when(has_lower)
            def _():
                down_to_lower(index).start()

            @pl.when(has_upper)
            def _():
                down_to_upper(index).start()

    def chain_down(index):
        @pl.when(t < root)
        def _():
            down_to_lower(index).wait_recv()

            @pl.when(has_lower)
            def _():
                down_to_lower(index).start()

        @pl.when(t > root)
        def _():
            down_to_upper(index).wait_recv()

            @pl.when(has_upper)
            def _():
                down_to_upper(index).start()

        down_to_sibling(index).start()
        target = pl.ds(pl.multiple_of(r * half + index * chunk, chunk), chunk)
        rows = part_rows(index)
        probe_out[0, 0, target, :] = down[rows, :points]
        probe_out[0, 1, target, :] = down[rows, points:]

    ends = (t == 0) | (t == tiles - 1)
    lag = CHAIN_LAG * jnp.abs(t - root)
    chain_steps = CHAIN_PARTS + CHAIN_LAG * max(root, tiles - 1 - root)

    def chain(start, stop):
        @pl.loop(start, stop)
        def _(index):
            @pl.when((index < CHAIN_PARTS) & jnp.logical_not(ends & (t != root)))
            def _():
                chain_up(index)

            @pl.when((index >= lag) & (index < lag + CHAIN_PARTS))
            def _():
                chain_down(index - lag)

    place = lax.broadcasted_iota(jnp.int32, (points, width), 1) - lax.broadcasted_iota(
        jnp.int32, (points, width), 0
    )
    place = jnp.where(place == col_start, 1.0, 0.0).astype(BF16)
    line = lax.broadcasted_iota(jnp.int32, (height, width), 0) + own_slot * height

    def send_placed(part):
        return copy(
            placed_out.at[part], placed_in.at[part], pl_send.at[part], pl_recv.at[part], sibling
        )

    def send_carry(part):
        return copy(carry_out.at[part], carry_in.at[part], c_send.at[part], c_recv.at[part], upper)

    def object_part(part):
        for which, target in ((1 - r, placed_out), (r, placed_mine)):
            send_term(which, part).wait()
            total = term[2 * m + which, part].astype(F32) + term_in[which, part].astype(F32)
            target[part] = matmul(total.astype(BF16), place).astype(BF16)
            if target is placed_out:
                send_placed(part).start()
        send_placed(part).wait()
        shift = shift_in[0:1, :]
        shift = jnp.broadcast_to(jnp.concatenate([shift] * (width // 128), 1), (height, width))
        zero = jnp.zeros((height, width), F32)
        mine, theirs = placed_mine[part].astype(F32), placed_in[part].astype(F32)
        carry_out[part] = (
            jnp.where(line < row_start, mine, zero) + jnp.where(line < shift, theirs, zero)
        ).astype(BF16)

        @pl.when(has_upper)
        def _():
            send_carry(part).start()

        own_sum[part] = jnp.where(line >= row_start, mine, zero) + jnp.where(
            line >= shift, theirs, zero
        )

    @pl.when(ends & (t != root))
    def _():
        @pl.loop(0, CHAIN_PARTS)
        def _(index):
            chain_up(index)

    chain(0, 6)
    send_shift.wait()
    object_part(0)
    chain(6, 13)
    object_part(1)
    chain(13, chain_steps)

    @pl.loop(0, CHAIN_PARTS)
    def _(index):
        down_to_sibling(index).wait()

        @pl.when(t < root)
        def _():
            up_to_upper(index).wait_send()

        @pl.when(t > root)
        def _():
            up_to_lower(index).wait_send()

        @pl.when((t <= root) & has_lower)
        def _():
            down_to_lower(index).wait_send()

        @pl.when((t >= root) & has_upper)
        def _():
            down_to_upper(index).wait_send()

    target = rows_at((1 - r) * half, half)
    probe_out[0, 0, target, :] = down_in[:, :points]
    probe_out[0, 1, target, :] = down_in[:, points:]

    for part in range(2):
        @pl.when(has_lower)
        def _():
            send_carry(part).wait_recv()
            object_out[part] = (own_sum[part] + carry_in[part].astype(F32)).astype(BF16)

        @pl.when(jnp.logical_not(has_lower))
        def _():
            object_out[part] = own_sum[part].astype(BF16)

        @pl.when(has_upper)
        def _():
            send_carry(part).wait_send()


def fused_local(tiles, object_tiles, probe_modes, measured, row_offset, col_offset):
    points = probe_modes.shape[-1]
    height, width = object_tiles.shape[1:]
    cosine, sine = (jnp.asarray(table) for table in cos_sin_tables(points))
    double, half = 2 * points, points // 2
    steps = points // POWER_ROWS
    vmem, smem = pl.BlockSpec(memory_space=pltpu.VMEM), pl.BlockSpec(memory_space=pltpu.SMEM)
    dma = pltpu.SemaphoreType.DMA
    scratch = [
        pltpu.VMEM(probe_modes.shape, BF16),
        pltpu.VMEM((points, points), BF16),
        pltpu.VMEM((points, points), BF16),
        pltpu.VMEM(measured.shape, F32),
        pltpu.VMEM((8, 2, height, width), BF16),
        pltpu.VMEM((8, 128), jnp.int32),
        pltpu.VMEM((8, 128), jnp.int32),
        pltpu.VMEM((points, points), BF16),
        pltpu.VMEM((points, points), BF16),
        pltpu.VMEM((double, double), BF16),
        pltpu.VMEM((double, double), BF16),
        pltpu.VMEM((double, double), BF16),
        pltpu.VMEM((double, double), BF16),
        pltpu.VMEM((2, points, points), BF16),
        pltpu.VMEM((2, points, points), BF16),
        pltpu.VMEM((double, points), BF16),
        pltpu.VMEM((points, double), BF16),
        pltpu.VMEM((points, double), F32),
        pltpu.VMEM((steps, POWER_ROWS, points), BF16),
        pltpu.VMEM((steps, POWER_ROWS, points), BF16),
        pltpu.VMEM((double, points), BF16),
        pltpu.VMEM((4, 2, height, points), BF16),
        pltpu.VMEM((2, 2, height, points), BF16),
        pltpu.VMEM((points, double), BF16),
        pltpu.VMEM((half, double), BF16),
        pltpu.VMEM((half, double), BF16),
        pltpu.VMEM((half, double), F32),
        pltpu.VMEM((half, double), BF16),
        pltpu.VMEM((half, double), BF16),
        pltpu.VMEM((half, double), BF16),
        pltpu.VMEM((half, double), BF16),
        pltpu.VMEM((half, double), BF16),
        pltpu.VMEM((2, height, width), BF16),
        pltpu.VMEM((2, height, width), BF16),
        pltpu.VMEM((2, height, width), BF16),
        pltpu.VMEM((2, height, width), BF16),
        pltpu.VMEM((2, height, width), BF16),
        pltpu.VMEM((2, height, width), F32),
        dma((7, GATHER_PARTS)), dma((7, GATHER_PARTS)), dma, dma, dma((steps,)), dma((steps,)), dma((2, 2)), dma((2, 2)),
        dma, dma, dma((5,)), dma((CHAIN_PARTS,)), dma((2, CHAIN_PARTS)), dma((2, CHAIN_PARTS)),
        dma((CHAIN_PARTS,)), dma((CHAIN_PARTS,)), dma((CHAIN_PARTS,)), dma((2,)), dma((2,)), dma((2,)), dma((2,)),
    ]
    object_grad, probe_grad = pl.pallas_call(
        functools.partial(fused_kernel, tiles),
        out_shape=(
            jax.ShapeDtypeStruct((2, height, width), BF16),
            jax.ShapeDtypeStruct((1, 2, points, points), BF16),
        ),
        in_specs=[smem, smem] + [pl.BlockSpec(memory_space=pl.ANY)] * 5,
        out_specs=(vmem, vmem),
        scratch_shapes=scratch,
        compiler_params=pltpu.CompilerParams(
            collective_id=0, has_side_effects=True, vmem_limit_bytes=56 * 1024 * 1024
        ),
    )(row_offset, col_offset, object_tiles, probe_modes, cosine, sine, measured)
    return object_grad.astype(F32), probe_grad.astype(F32)


def solution(mesh):
    placed = (
        P(None, ("groups", "tile", "mode", "rep"), None),
        P(("groups", "mode"), None, None, None),
        P(("groups", "tile", "rep"), None, None),
        P(("groups", "tile", "rep")),
        P(("groups", "tile", "rep")),
    )
    if mesh.shape["mode"] == 2 and mesh.shape["rep"] == 2:
        body = functools.partial(fused_local, mesh.shape["tile"])
    else:
        body = local
    return jax.shard_map(
        body,
        mesh=mesh,
        in_specs=placed,
        out_specs=(
            P(None, ("groups", "tile", "mode", "rep"), None),
            P(("groups", "mode"), None, None, None),
        ),
        check_vma=False,
    )
```

```python
import functools
import math

import jax
import jax.numpy as jnp
import numpy as np
from jax import lax
from jax.experimental import pallas as pl
from jax.experimental.pallas import tpu as pltpu
from jax.sharding import PartitionSpec as P

PATCH = 512
F32, BF16 = jnp.float32, jnp.bfloat16
POWER_ROWS = 128
CHAIN_PARTS = 8
CHAIN_LAG = 5
IN_FLIGHT = 3
GATHER_PARTS = 4

def passed_along(value, axis, steps):
    count = lax.axis_size(axis)
    initial, last = (max(0, -steps), min(count, count - steps))
    return lax.ppermute(value, axis, [(source, source + steps) for source in range(initial, last)])


def dft_tables(points):
    indices = jnp.arange(points, dtype=jnp.int32)
    products = indices[:, None] * indices[None, :] % points
    angles = products.astype(jnp.float32) * (2.0 * math.pi / points)
    norm_factor = 1.0 / math.sqrt(points)
    cos_table = (jnp.cos(angles) * norm_factor).astype(jnp.bfloat16)
    sin_table = (jnp.sin(angles) * norm_factor).astype(jnp.bfloat16)
    forward_left = jnp.concatenate(
        [jnp.concatenate([cos_table, sin_table], 1), jnp.concatenate([-sin_table, cos_table], 1)], 0
    )
    inverse_left = jnp.concatenate(
        [jnp.concatenate([cos_table, -sin_table], 1), jnp.concatenate([sin_table, cos_table], 1)], 0
    )
    return (cos_table, sin_table, forward_left, inverse_left)


def column_pass(left_matrix, stacked):
    points = stacked.shape[-1]
    product = jnp.dot(
        left_matrix, stacked.reshape(2 * points, points), preferred_element_type=jnp.float32
    )
    return product.reshape(2, points, points)


def row_pass(stacked, cos_table, sin_table, sign_flip):
    points = stacked.shape[-1]
    flattened = stacked.reshape(2 * points, points)
    with_cos = jnp.dot(flattened, cos_table, preferred_element_type=jnp.float32).reshape(
        2, points, points
    )
    with_sin = jnp.dot(flattened, sin_table, preferred_element_type=jnp.float32).reshape(
        2, points, points
    )
    real_part = with_cos[0] + sign_flip * with_sin[1]
    imag_part = with_cos[1] - sign_flip * with_sin[0]
    return jnp.stack([real_part, imag_part])


def forward_wave(exit_wave, tables):
    cos_table, sin_table, forward_left, inverse_left = tables
    middle = column_pass(forward_left, exit_wave).astype(jnp.bfloat16)
    return row_pass(middle, cos_table, sin_table, 1.0)


def inverse_wave(corrected, tables):
    cos_table, sin_table, forward_left, inverse_left = tables
    middle = column_pass(inverse_left, corrected).astype(jnp.bfloat16)
    return row_pass(middle, cos_table, sin_table, -1.0)


def complex_times(first, second):
    real_part = first[0] * second[0] - first[1] * second[1]
    imag_part = first[0] * second[1] + first[1] * second[0]
    return jnp.stack([real_part, imag_part])


def conj_times(first, second):
    real_part = first[0] * second[0] + first[1] * second[1]
    imag_part = first[0] * second[1] - first[1] * second[0]
    return jnp.stack([real_part, imag_part])


def local(object_tiles, probe_modes, measured, row_offset, col_offset):
    tables = dft_tables(PATCH)
    own_rows = lax.all_gather(object_tiles, ("mode", "rep"), axis=1, tiled=True)
    next_rows = passed_along(own_rows, "tile", -1)
    extended = jnp.concatenate([own_rows, next_rows], axis=1)
    tile_rows = own_rows.shape[1]
    obj_cols = extended.shape[2]
    zero_index = jnp.zeros((), jnp.int32)
    row_start = row_offset[0]
    col_start = col_offset[0]
    obj_patch = lax.dynamic_slice(
        extended, (zero_index, row_start, col_start), (2, PATCH, PATCH)
    ).astype(jnp.float32)
    probe_float = probe_modes[0].astype(jnp.float32)
    exit_wave = complex_times(probe_float, obj_patch).astype(jnp.bfloat16)
    spectra = forward_wave(exit_wave, tables)
    local_power = spectra[0] ** 2 + spectra[1] ** 2
    intensity = lax.psum(local_power.astype(jnp.bfloat16), "mode").astype(jnp.float32)
    factor = 1.0 - measured[0] / jnp.sqrt(jnp.maximum(intensity, 1.0))
    corrected = (spectra * factor).astype(jnp.bfloat16)
    back_wave = inverse_wave(corrected, tables)
    obj_term = conj_times(probe_float, back_wave).astype(jnp.bfloat16).astype(jnp.float32)
    extended_term = jnp.zeros((2, 2 * tile_rows, obj_cols), jnp.float32)
    extended_term = lax.dynamic_update_slice(
        extended_term, obj_term, (zero_index, row_start, col_start)
    )
    own_sum, next_sum = (
        lax.psum_scatter(
            extended_term[:, :tile_rows].astype(jnp.bfloat16),
            ("mode", "rep"),
            scatter_dimension=1,
            tiled=True,
        ).astype(jnp.float32),
        lax.psum_scatter(
            extended_term[:, tile_rows:].astype(jnp.bfloat16),
            ("mode", "rep"),
            scatter_dimension=1,
            tiled=True,
        ).astype(jnp.float32),
    )
    carried = passed_along(next_sum.astype(jnp.bfloat16), "tile", 1).astype(next_sum.dtype)
    object_grad = own_sum + carried
    probe_term = conj_times(obj_patch, back_wave)
    probe_grad = lax.psum(probe_term.astype(jnp.bfloat16), ("tile", "rep")).astype(jnp.float32)
    return (object_grad, probe_grad[None])


def cos_sin_tables(points):
    products = np.outer(np.arange(points), np.arange(points)) % points
    angles = products * (2.0 * math.pi / points)
    norm_factor = 1.0 / math.sqrt(points)
    return (
        (np.cos(angles) * norm_factor).astype(jnp.bfloat16),
        (np.sin(angles) * norm_factor).astype(jnp.bfloat16),
    )


def matmul(left, right):
    return jnp.dot(left, right, preferred_element_type=F32)


def rows_at(start, size):
    return pl.ds(pl.multiple_of(start, size), size)


def fused_kernel(
    tiles, row_ref, col_ref, obj, probe_hbm, cos_hbm, sin_hbm, measured_hbm, object_out, probe_out,
    probe, cos_ref, sin_ref, measured,
    ext, shift_out, shift_in, rotate, rotate_back, left_fwd, right_fwd, right_inv, left_inv,
    probe_rot, patch, wave, middle, spec, power, power_in, back_stack, term, term_in,
    probe_term, half_out, half_in, half_sum, up_left, up_right, up_out, down, down_in,
    placed_out, placed_mine, placed_in, carry_out, carry_in, own_sum,
    g_send, g_recv, s_send, s_recv, pw_send, pw_recv, t_send, t_recv, h_send, h_recv, load,
    up_send, up_recv, dn_send, dn_recv, sib_send, sib_recv, pl_send, pl_recv, c_send, c_recv,
):
    t, m, r = lax.axis_index("tile"), lax.axis_index("mode"), lax.axis_index("rep")
    sibling, partner = {"rep": 1 - r}, {"mode": 1 - m}
    lower, upper = {"tile": t - 1}, {"tile": t + 1}
    has_lower, has_upper = t > 0, t < tiles - 1
    height, width = obj.shape[1], obj.shape[2]
    points = probe.shape[-1]
    piece = 2 * height // GATHER_PARTS
    row_start, col_start = row_ref[0], col_ref[0]

    def copy(src, dst, send, recv, device):
        return pltpu.make_async_remote_copy(
            src_ref=src, dst_ref=dst, send_sem=send, recv_sem=recv,
            device_id=device, device_id_type=pl.DeviceIdType.MESH,
        )

    own_slot, other_slot = 2 * m + r, 2 * (1 - m) + r
    loads = [
        pltpu.make_async_copy(src, dst, load.at[index])
        for index, (src, dst) in enumerate(
            (
                (probe_hbm, probe), (cos_hbm, cos_ref), (sin_hbm, sin_ref),
                (measured_hbm, measured), (obj, ext.at[own_slot]),
            )
        )
    ]
    for one in loads:
        one.start()

    barrier = pltpu.get_barrier_semaphore()
    for device in (sibling, partner):
        pl.semaphore_signal(barrier, inc=1, device_id=device, device_id_type=pl.DeviceIdType.MESH)

    @pl.when(has_lower)
    def _():
        pl.semaphore_signal(barrier, inc=1, device_id=lower, device_id_type=pl.DeviceIdType.MESH)

    @pl.when(has_upper)
    def _():
        pl.semaphore_signal(barrier, inc=1, device_id=upper, device_id_type=pl.DeviceIdType.MESH)

    peers = 2 + has_lower.astype(jnp.int32) + has_upper.astype(jnp.int32)
    pl.semaphore_wait(barrier, peers)


    def lines(part):
        return part // (GATHER_PARTS // 2), pl.ds(part % (GATHER_PARTS // 2) * piece, piece)

    def gather(kind, part, src, slot, device):
        return copy(src, ext.at[slot, *lines(part)], g_send.at[kind, part], g_recv.at[kind, part], device)

    def block(slot, part):
        return ext.at[slot, *lines(part)]

    def to_sibling(part):
        return gather(0, part, obj.at[*lines(part)], own_slot, sibling)

    def to_partner(part):
        return gather(1, part, obj.at[*lines(part)], own_slot, partner)

    def to_lower(part):
        return gather(2, part, obj.at[*lines(part)], 4 + own_slot, lower)

    def relay_partner(part):
        return gather(3, part, block(other_slot, part), other_slot, sibling)

    def relay_upper(part):
        return gather(4, part, block(4 + own_slot, part), 4 + own_slot, sibling)

    def cross_partner(part):
        return gather(5, part, block(4 + own_slot, part), 4 + own_slot, partner)

    def cross_lower(part):
        return gather(5, part, block(other_slot, part), 4 + other_slot, lower)

    def relay_cross(part):
        return gather(6, part, block(4 + other_slot, part), 4 + other_slot, sibling)

    for part in range(GATHER_PARTS):
        to_partner(part).start()

        @pl.when(has_lower)
        def _():
            to_lower(part).start()

        to_sibling(part).start()
    shift_out[...] = jnp.full(shift_out.shape, row_start, jnp.int32)
    send_shift = copy(shift_out, shift_in, s_send, s_recv, sibling)
    send_shift.start()

    first = lax.broadcasted_iota(jnp.int32, (points, points), 0)
    second = lax.broadcasted_iota(jnp.int32, (points, points), 1)
    apart = first - second - row_start
    rotate[...] = jnp.where((apart == 0) | (apart == -points), 1.0, 0.0).astype(BF16)
    apart = second - first - row_start
    rotate_back[...] = jnp.where((apart == 0) | (apart == -points), 1.0, 0.0).astype(BF16)
    for one in loads[:3]:
        one.wait()
    cosine, sine = cos_ref[...], sin_ref[...]
    minus = -sine
    right_fwd[:points, :points] = cosine
    right_fwd[:points, points:] = minus
    right_fwd[points:, :points] = sine
    right_fwd[points:, points:] = cosine
    right_inv[:points, :points] = cosine
    right_inv[:points, points:] = sine
    right_inv[points:, :points] = minus
    right_inv[points:, points:] = cosine

    @pl.loop(0, 4)
    def _(step):
        rows = rows_at(step * 128, 128)
        low = rows_at(points + step * 128, 128)
        turn = rotate[rows, :]
        cos_rot = matmul(turn, cos_ref[...]).astype(BF16)
        sin_rot = matmul(turn, sin_ref[...]).astype(BF16)
        left_inv[rows, :points] = cos_rot
        left_inv[rows, points:] = -sin_rot
        left_inv[low, :points] = sin_rot
        left_inv[low, points:] = cos_rot
        cos_turn = matmul(cos_ref[rows, :], rotate_back[...]).astype(BF16)
        sin_turn = matmul(sin_ref[rows, :], rotate_back[...]).astype(BF16)
        left_fwd[rows, :points] = cos_turn
        left_fwd[rows, points:] = sin_turn
        left_fwd[low, :points] = -sin_turn
        left_fwd[low, points:] = cos_turn
        for part in range(2):
            probe_rot[part, rows, :] = matmul(turn, probe[0, part]).astype(BF16)

    for one in loads[3:]:
        one.wait()

    @pl.when(jnp.logical_not(has_upper))
    def _():
        ext[4:8] = jnp.zeros((4, 2, height, width), BF16)

    @pl.when(t == 0)
    def _():
        up_left[...] = jnp.zeros_like(up_left)

    @pl.when(t == tiles - 1)
    def _():
        up_right[...] = jnp.zeros_like(up_right)

    for part in range(GATHER_PARTS):
        gather(1, part, obj.at[*lines(part)], other_slot, partner).wait_recv()
        relay_partner(part).start()

        @pl.when((r == 1) & has_lower)
        def _():
            cross_lower(part).start()

        @pl.when(has_upper)
        def _():
            gather(2, part, obj.at[*lines(part)], 4 + own_slot, lower).wait_recv()
            relay_upper(part).start()

            @pl.when(r == 0)
            def _():
                cross_partner(part).start()

    for part in range(GATHER_PARTS):
        to_sibling(part).wait_recv()

        @pl.when(has_upper)
        def _():
            relay_upper(part).wait_recv()

    pick = lax.broadcasted_iota(jnp.int32, (width, points), 0) - lax.broadcasted_iota(
        jnp.int32, (width, points), 1
    )
    pick = jnp.where(pick == col_start, 1.0, 0.0).astype(BF16)

    def exit_rows(side):
        @pl.loop(0, 2)
        def _(index):
            step = 2 * side + index
            rows = rows_at(step * height, height)
            low = rows_at(points + step * height, height)
            line = lax.broadcasted_iota(jnp.int32, (height, width), 0) + step * height
            parts = []
            for part in range(2):
                chosen = jnp.where(
                    line >= row_start, ext[step, part].astype(F32), ext[4 + step, part].astype(F32)
                )
                parts.append(matmul(chosen.astype(BF16), pick))
                patch[part, rows, :] = parts[part].astype(BF16)
            obj_re, obj_im = parts
            prb_re, prb_im = (probe_rot[part, rows, :].astype(F32) for part in range(2))
            wave[rows, :] = (prb_re * obj_re - prb_im * obj_im).astype(BF16)
            wave[low, :] = (prb_re * obj_im + prb_im * obj_re).astype(BF16)

    def column_part(rows, side):
        near = rows_at(2 * side * height, 2 * height)
        far = rows_at(points + 2 * side * height, 2 * height)
        return matmul(left_fwd[rows, near], wave[near, :]) + matmul(left_fwd[rows, far], wave[far, :])

    exit_rows(m)

    @pl.loop(0, 2)
    def _(step):
        rows = rows_at(step * 256, 256)
        low = rows_at(points + step * 256, 256)
        spec[rows, :points] = column_part(rows, m)
        spec[rows, points:] = column_part(low, m)

    for part in range(GATHER_PARTS):
        @pl.when(has_upper)
        def _():
            gather(5, part, obj.at[*lines(part)], 4 + other_slot, partner).wait_recv()
            relay_cross(part).start()

    for part in range(GATHER_PARTS):
        relay_partner(part).wait_recv()

        @pl.when(has_upper)
        def _():
            relay_cross(part).wait_recv()

    exit_rows(1 - m)

    @pl.loop(0, 2)
    def _(step):
        rows = rows_at(step * 256, 256)
        low = rows_at(points + step * 256, 256)
        middle[rows, :points] = (spec[rows, :points] + column_part(rows, 1 - m)).astype(BF16)
        middle[rows, points:] = (spec[rows, points:] + column_part(low, 1 - m)).astype(BF16)

    def send_power(step):
        return copy(
            power.at[step], power_in.at[step], pw_send.at[step], pw_recv.at[step], partner
        )

    steps = points // POWER_ROWS

    @pl.loop(0, steps)
    def _(step):
        rows = rows_at(step * POWER_ROWS, POWER_ROWS)
        wide = matmul(middle[rows, :], right_fwd[...])
        spec[rows, :] = wide
        power[step] = (wide[:, :points] ** 2 + wide[:, points:] ** 2).astype(BF16)

        @pl.when(step < IN_FLIGHT)
        def _():
            send_power(step).start()

    @pl.loop(0, steps)
    def _(step):
        rows = rows_at(step * POWER_ROWS, POWER_ROWS)
        low = rows_at(points + step * POWER_ROWS, POWER_ROWS)
        send_power(step).wait()

        @pl.when(step + IN_FLIGHT < steps)
        def _():
            send_power(step + IN_FLIGHT).start()

        spec_re, spec_im = spec[rows, :points], spec[rows, points:]
        intensity = spec_re**2 + spec_im**2 + power_in[step].astype(F32)
        factor = 1.0 - measured[0, rows, :] / jnp.sqrt(jnp.maximum(intensity, 1.0))
        corrected = jnp.concatenate(
            [(spec_re * factor).astype(BF16), (spec_im * factor).astype(BF16)], 1
        )
        turned = matmul(corrected, right_inv[...]).astype(BF16)
        back_stack[rows, :] = turned[:, :points]
        back_stack[low, :] = turned[:, points:]

    for part in range(GATHER_PARTS):
        to_sibling(part).wait_send()
        to_partner(part).wait_send()
        relay_partner(part).wait_send()

        @pl.when(has_lower)
        def _():
            to_lower(part).wait_send()

        @pl.when((r == 1) & has_lower)
        def _():
            cross_lower(part).wait_send()

        @pl.when(has_upper)
        def _():
            relay_upper(part).wait_send()
            relay_cross(part).wait_send()

        @pl.when((r == 0) & has_upper)
        def _():
            cross_partner(part).wait_send()

    def send_term(which, part):
        return copy(
            term.at[2 * (1 - m) + which, part], term_in.at[which, part],
            t_send.at[which, part], t_recv.at[which, part], partner,
        )

    @pl.loop(0, 4)
    def _(step):
        slot = (step + 2 * (1 - m)) % 4
        rows = rows_at(slot * height, height)
        low = rows_at(points + slot * height, height)
        back_re = matmul(left_inv[rows, :], back_stack[...])
        back_im = matmul(left_inv[low, :], back_stack[...])
        prb_re, prb_im = (probe_rot[part, rows, :].astype(F32) for part in range(2))
        term[slot, 0] = (prb_re * back_re + prb_im * back_im).astype(BF16)
        term[slot, 1] = (prb_re * back_im - prb_im * back_re).astype(BF16)

        @pl.when(step == 1)
        def _():
            for which in (1 - r, r):
                send_term(which, 0).start()

        obj_re, obj_im = (patch[part, rows, :].astype(F32) for part in range(2))
        probe_term[rows, :points] = (obj_re * back_re + obj_im * back_im).astype(BF16)
        probe_term[rows, points:] = (obj_re * back_im - obj_im * back_re).astype(BF16)

    half = points // 2
    chunk = half // CHAIN_PARTS
    half_out[...] = matmul(rotate_back[rows_at((1 - r) * half, half), :], probe_term[...]).astype(BF16)
    send_half = copy(half_out, half_in, h_send, h_recv, sibling)
    send_half.start()
    half_sum[...] = matmul(rotate_back[rows_at(r * half, half), :], probe_term[...])
    send_half.wait()
    half_sum[...] += half_in[...].astype(F32)
    root = tiles // 2

    def part_rows(index):
        return pl.ds(pl.multiple_of(index * chunk, chunk), chunk)

    def up_to_upper(index):
        rows = part_rows(index)
        return copy(up_out.at[rows], up_left.at[rows], up_send.at[index], up_recv.at[0, index], upper)

    def up_to_lower(index):
        rows = part_rows(index)
        return copy(up_out.at[rows], up_right.at[rows], up_send.at[index], up_recv.at[1, index], lower)

    def down_to_upper(index):
        rows = part_rows(index)
        return copy(down.at[rows], down.at[rows], dn_send.at[0, index], dn_recv.at[index], upper)

    def down_to_lower(index):
        rows = part_rows(index)
        return copy(down.at[rows], down.at[rows], dn_send.at[1, index], dn_recv.at[index], lower)

    def down_to_sibling(index):
        rows = part_rows(index)
        return copy(down.at[rows], down_in.at[rows], sib_send.at[index], sib_recv.at[index], sibling)

    def chain_up(index):
        rows = part_rows(index)

        @pl.when((t <= root) & has_lower)
        def _():
            up_to_upper(index).wait_recv()

        @pl.when((t >= root) & has_upper)
        def _():
            up_to_lower(index).wait_recv()

        @pl.when(t < root)
        def _():
            up_out[rows] = (half_sum[rows] + up_left[rows].astype(F32)).astype(BF16)

            @pl.when(index >= IN_FLIGHT)
            def _():
                up_to_upper(index - IN_FLIGHT).wait_send()

            up_to_upper(index).start()

        @pl.when(t > root)
        def _():
            up_out[rows] = (half_sum[rows] + up_right[rows].astype(F32)).astype(BF16)

            @pl.when(index >= IN_FLIGHT)
            def _():
                up_to_lower(index - IN_FLIGHT).wait_send()

            up_to_lower(index).start()

        @pl.when(t == root)
        def _():
            down[rows] = (
                half_sum[rows] + up_left[rows].astype(F32) + up_right[rows].astype(F32)
            ).astype(BF16)

            @pl.when(has_lower)
            def _():
                down_to_lower(index).start()

            @pl.when(has_upper)
            def _():
                down_to_upper(index).start()

    def chain_down(index):
        @pl.when(t < root)
        def _():
            down_to_lower(index).wait_recv()

            @pl.when(has_lower)
            def _():
                down_to_lower(index).start()

        @pl.when(t > root)
        def _():
            down_to_upper(index).wait_recv()

            @pl.when(has_upper)
            def _():
                down_to_upper(index).start()

        down_to_sibling(index).start()
        target = pl.ds(pl.multiple_of(r * half + index * chunk, chunk), chunk)
        rows = part_rows(index)
        probe_out[0, 0, target, :] = down[rows, :points]
        probe_out[0, 1, target, :] = down[rows, points:]

    lag = CHAIN_LAG * jnp.abs(t - root)
    chain_steps = CHAIN_PARTS + CHAIN_LAG * max(root, tiles - 1 - root)

    def chain(start, stop):
        @pl.loop(start, stop)
        def _(index):
            @pl.when(index < CHAIN_PARTS)
            def _():
                chain_up(index)

            @pl.when((index >= lag) & (index < lag + CHAIN_PARTS))
            def _():
                chain_down(index - lag)

    place = lax.broadcasted_iota(jnp.int32, (points, width), 1) - lax.broadcasted_iota(
        jnp.int32, (points, width), 0
    )
    place = jnp.where(place == col_start, 1.0, 0.0).astype(BF16)
    line = lax.broadcasted_iota(jnp.int32, (height, width), 0) + own_slot * height

    def send_placed(part):
        return copy(
            placed_out.at[part], placed_in.at[part], pl_send.at[part], pl_recv.at[part], sibling
        )

    def send_carry(part):
        return copy(carry_out.at[part], carry_in.at[part], c_send.at[part], c_recv.at[part], upper)

    def object_part(part):
        for which, target in ((1 - r, placed_out), (r, placed_mine)):
            send_term(which, part).wait()
            total = term[2 * m + which, part].astype(F32) + term_in[which, part].astype(F32)
            target[part] = matmul(total.astype(BF16), place).astype(BF16)
            if target is placed_out:
                send_placed(part).start()
        send_placed(part).wait()
        shift = shift_in[0:1, :]
        shift = jnp.broadcast_to(jnp.concatenate([shift] * (width // 128), 1), (height, width))
        zero = jnp.zeros((height, width), F32)
        mine, theirs = placed_mine[part].astype(F32), placed_in[part].astype(F32)
        carry_out[part] = (
            jnp.where(line < row_start, mine, zero) + jnp.where(line < shift, theirs, zero)
        ).astype(BF16)

        @pl.when(has_upper)
        def _():
            send_carry(part).start()

        own_sum[part] = jnp.where(line >= row_start, mine, zero) + jnp.where(
            line >= shift, theirs, zero
        )

    chain(0, 2)
    for which in (1 - r, r):
        send_term(which, 1).start()
    chain(2, CHAIN_PARTS)
    send_shift.wait()
    object_part(0)
    chain(CHAIN_PARTS, CHAIN_PARTS + 1)
    object_part(1)
    chain(CHAIN_PARTS + 1, chain_steps)

    @pl.loop(0, CHAIN_PARTS)
    def _(index):
        down_to_sibling(index).wait()

        @pl.when((t < root) & (index >= CHAIN_PARTS - IN_FLIGHT))
        def _():
            up_to_upper(index).wait_send()

        @pl.when((t > root) & (index >= CHAIN_PARTS - IN_FLIGHT))
        def _():
            up_to_lower(index).wait_send()

        @pl.when((t <= root) & has_lower)
        def _():
            down_to_lower(index).wait_send()

        @pl.when((t >= root) & has_upper)
        def _():
            down_to_upper(index).wait_send()

    target = rows_at((1 - r) * half, half)
    probe_out[0, 0, target, :] = down_in[:, :points]
    probe_out[0, 1, target, :] = down_in[:, points:]

    for part in range(2):
        @pl.when(has_lower)
        def _():
            send_carry(part).wait_recv()
            object_out[part] = (own_sum[part] + carry_in[part].astype(F32)).astype(BF16)

        @pl.when(jnp.logical_not(has_lower))
        def _():
            object_out[part] = own_sum[part].astype(BF16)

        @pl.when(has_upper)
        def _():
            send_carry(part).wait_send()


def fused_local(tiles, object_tiles, probe_modes, measured, row_offset, col_offset):
    points = probe_modes.shape[-1]
    height, width = object_tiles.shape[1:]
    cosine, sine = (jnp.asarray(table) for table in cos_sin_tables(points))
    double, half = 2 * points, points // 2
    steps = points // POWER_ROWS
    vmem, smem = pl.BlockSpec(memory_space=pltpu.VMEM), pl.BlockSpec(memory_space=pltpu.SMEM)
    dma = pltpu.SemaphoreType.DMA
    scratch = [
        pltpu.VMEM(probe_modes.shape, BF16),
        pltpu.VMEM((points, points), BF16),
        pltpu.VMEM((points, points), BF16),
        pltpu.VMEM(measured.shape, F32),
        pltpu.VMEM((8, 2, height, width), BF16),
        pltpu.VMEM((8, 128), jnp.int32),
        pltpu.VMEM((8, 128), jnp.int32),
        pltpu.VMEM((points, points), BF16),
        pltpu.VMEM((points, points), BF16),
        pltpu.VMEM((double, double), BF16),
        pltpu.VMEM((double, double), BF16),
        pltpu.VMEM((double, double), BF16),
        pltpu.VMEM((double, double), BF16),
        pltpu.VMEM((2, points, points), BF16),
        pltpu.VMEM((2, points, points), BF16),
        pltpu.VMEM((double, points), BF16),
        pltpu.VMEM((points, double), BF16),
        pltpu.VMEM((points, double), F32),
        pltpu.VMEM((steps, POWER_ROWS, points), BF16),
        pltpu.VMEM((steps, POWER_ROWS, points), BF16),
        pltpu.VMEM((double, points), BF16),
        pltpu.VMEM((4, 2, height, points), BF16),
        pltpu.VMEM((2, 2, height, points), BF16),
        pltpu.VMEM((points, double), BF16),
        pltpu.VMEM((half, double), BF16),
        pltpu.VMEM((half, double), BF16),
        pltpu.VMEM((half, double), F32),
        pltpu.VMEM((half, double), BF16),
        pltpu.VMEM((half, double), BF16),
        pltpu.VMEM((half, double), BF16),
        pltpu.VMEM((half, double), BF16),
        pltpu.VMEM((half, double), BF16),
        pltpu.VMEM((2, height, width), BF16),
        pltpu.VMEM((2, height, width), BF16),
        pltpu.VMEM((2, height, width), BF16),
        pltpu.VMEM((2, height, width), BF16),
        pltpu.VMEM((2, height, width), BF16),
        pltpu.VMEM((2, height, width), F32),
        dma((7, GATHER_PARTS)), dma((7, GATHER_PARTS)), dma, dma, dma((steps,)), dma((steps,)), dma((2, 2)), dma((2, 2)),
        dma, dma, dma((5,)), dma((CHAIN_PARTS,)), dma((2, CHAIN_PARTS)), dma((2, CHAIN_PARTS)),
        dma((CHAIN_PARTS,)), dma((CHAIN_PARTS,)), dma((CHAIN_PARTS,)), dma((2,)), dma((2,)), dma((2,)), dma((2,)),
    ]
    object_grad, probe_grad = pl.pallas_call(
        functools.partial(fused_kernel, tiles),
        out_shape=(
            jax.ShapeDtypeStruct((2, height, width), BF16),
            jax.ShapeDtypeStruct((1, 2, points, points), BF16),
        ),
        in_specs=[smem, smem] + [pl.BlockSpec(memory_space=pl.ANY)] * 5,
        out_specs=(vmem, vmem),
        scratch_shapes=scratch,
        compiler_params=pltpu.CompilerParams(
            collective_id=0, has_side_effects=True, vmem_limit_bytes=56 * 1024 * 1024
        ),
    )(row_offset, col_offset, object_tiles, probe_modes, cosine, sine, measured)
    return object_grad.astype(F32), probe_grad.astype(F32)


def solution(mesh):
    placed = (
        P(None, ("groups", "tile", "mode", "rep"), None),
        P(("groups", "mode"), None, None, None),
        P(("groups", "tile", "rep"), None, None),
        P(("groups", "tile", "rep")),
        P(("groups", "tile", "rep")),
    )
    if mesh.shape["mode"] == 2 and mesh.shape["rep"] == 2:
        body = functools.partial(fused_local, mesh.shape["tile"])
    else:
        body = local
    return jax.shard_map(
        body,
        mesh=mesh,
        in_specs=placed,
        out_specs=(
            P(None, ("groups", "tile", "mode", "rep"), None),
            P(("groups", "mode"), None, None, None),
        ),
        check_vma=False,
    )
```
